256 devices in a mesh: dp: 4 (over z_hi), ctx: 8 (over y, core), head: 8 (over z_lo, x).
Axes of the slice: x: 4, y: 4, z: 8 (z_hi: 4, z_lo: 2; z = z_hi * 2 + z_lo), core: 2. Of those that a mesh axis runs over, the one named last changes fastest.
Arguments:
- q_nope: bfloat16 [4, 1024, 8192], P('dp', 'ctx', 'head'), may hold values from -6 to 6
- q_rope: bfloat16 [4, 1024, 4096], P('dp', 'ctx', 'head'), may hold values from -7.5 to 7.5
- kv_latent: bfloat16 [4, 1024, 576], P('dp', 'ctx'), may hold values from -7.5 to 7.5
- d_out: bfloat16 [4, 1024, 8192], P('dp', 'ctx', 'head'), may hold values from -6 to 6
- w_uk: bfloat16 [512, 8192], P(None, 'head'), may hold values from -0.25 to 0.25
- w_uv: bfloat16 [512, 8192], P(None, 'head'), may hold values from -0.25 to 0.25
- segment_ids: int32 [4, 1024], P('dp'), may hold values from 0 to 3, never falling along the last dimension, each value on 1 to 512 neighbouring positions
- span_order: int32 [16], replicated, may hold values from 0 to 15, as said below
Outputs:
- dq_nope: bfloat16 [4, 1024, 8192], P('dp', 'ctx', 'head')
- dq_rope: bfloat16 [4, 1024, 4096], P('dp', 'ctx', 'head')
- d_kv: bfloat16 [4, 1024, 576], P('dp', ('ctx', 'head'))
- dw_uk: float32 [512, 8192], P(None, 'head')
- dw_uv: float32 [512, 8192], P(None, 'head')
The draws below stay inside these ranges and needn't reach their ends.
Inputs may be any that keep to these rules, and one draw needn't show every extreme that they name: `span_order`: a permutation of the 16 span numbers in which storage slots 2 c and 2 c + 1 hold two spans whose numbers add up to 15.
All inputs are finite; a program needn't handle non-finite values.
Results may differ from the reference program's by a relative error of at most 0.03.
Values may be sent and summed in bfloat16 or wider, within the bound.
No kernel may reach another device: no remote copies, remote signals or barrier semaphores. Data moves between devices by JAX's collectives and lax.ppermute only.
A program may use at most 64 MiB of HBM per device.

```python
import math
import jax
import jax.numpy as jnp
import numpy as np
from jax import lax

LAT = 512
ROPE = 64
NOPE = 128
VDIM = 128
SEGS = 4
HEADS = 64
SEQ = 1024
SPANS = 16
ROLLOUTS = 4


def draw_kv_latent(key, part):
    key = jax.random.fold_in(key, 11)
    base = jax.random.normal(key, (ROLLOUTS, SEQ, LAT + ROPE), jnp.float32)
    return jnp.clip(base, -6.0, 6.0).astype(jnp.bfloat16)


def draw_q_rope(key, part):
    key = jax.random.fold_in(key, 23)
    base = jax.random.normal(key, (ROLLOUTS, SEQ, HEADS * ROPE), jnp.float32)
    return jnp.clip(base, -6.0, 6.0).astype(jnp.bfloat16)


def draw_span_order(key, part):
    key = jax.random.fold_in(key, 37)
    pairs = SPANS // 2
    shuffled = jax.random.permutation(jax.random.fold_in(key, 1), pairs).astype(jnp.int32)
    flips = jax.random.randint(jax.random.fold_in(key, 2), (pairs,), 0, 2)
    lower = jnp.where(flips == 1, shuffled, SPANS - 1 - shuffled)
    upper = SPANS - 1 - lower
    return jnp.stack([lower, upper], axis=1).reshape(SPANS).astype(jnp.int32)


def block_levels(stream_key, extent, cuts, smallest, top_value):
    gain, own = 1.0, jax.random.fold_in(stream_key, 6)
    for position, blocks in cuts:
        heights = jnp.exp(jax.random.uniform(jax.random.fold_in(own, position), (blocks,), jnp.float32, smallest / len(cuts), top_value / len(cuts)))
        gain = gain * jnp.repeat(heights, extent[position] // blocks).reshape([-1 if axis == position else 1 for axis in range(len(extent))])
    return gain


def length_profile(amount, total, limit, slope):
    portions = [(1 << 20) // math.isqrt(grade ** slope) + 1 for grade in range(2, amount + 1)]
    spare, given = total - limit - (amount - 1), [1] * (amount - 1)
    while spare > 0:
        free = [i for i in range(amount - 1) if given[i] < limit]
        whole, budget = sum([portions[i] for i in free]), spare
        for i in free:
            extra = min(limit - given[i], max(1, budget * portions[i] // whole), spare)
            given[i] = given[i] + extra
            spare = spare - extra
    return np.array([limit] + given)


def uneven(own_key, number_of, total, limit, lean):
    if number_of == 2:
        one = jax.random.randint(own_key, (), max(1, total - limit), min(limit, total - 1) + 1)
        return jnp.stack([one, total - one])
    tallies = jnp.asarray(length_profile(number_of, total, limit, lean), jnp.int32)
    pairs = (number_of - 1) // 2
    donor, sink = tallies[1:1 + 2 * pairs:2], tallies[2:2 + 2 * pairs:2]
    room = jnp.minimum(donor - 1, limit - sink)
    passed = jax.random.randint(jax.random.fold_in(own_key, 1), (pairs,), 0, 1 << 20) % (room + 1)
    tallies = tallies.at[1:1 + 2 * pairs:2].set(donor - passed).at[2:2 + 2 * pairs:2].set(sink + passed)
    return tallies[jax.random.permutation(jax.random.fold_in(own_key, 2), number_of)]


def centred(own_key, shape, deviation, limit, shards=(), held_as=jnp.bfloat16):
    factor_of = block_levels(own_key, shape, shards, -0.22, 0.18) if shards else 1.0
    drawn = jax.random.normal(own_key, shape, jnp.float32) * deviation * factor_of
    return jnp.minimum(jnp.maximum(drawn, -limit), limit).astype(held_as)


def setup_inputs(seed: int = 0) -> dict:
    streams_of = jax.random.split(jax.random.key(seed), 9)
    q_nope = centred(streams_of[0], (ROLLOUTS, SEQ, HEADS * NOPE), 1.0, 6.0, ((0, 4), (1, 8), (2, 8)))
    q_rope = draw_q_rope(jax.random.fold_in(streams_of[8], 71), 0)
    kv_latent = draw_kv_latent(jax.random.fold_in(streams_of[8], 71), 0)
    d_out = centred(streams_of[3], (ROLLOUTS, SEQ, HEADS * VDIM), 1.0, 6.0, ((0, 4), (1, 8), (2, 8)))
    w_uk = centred(streams_of[4], (LAT, HEADS * NOPE), LAT ** -0.5, 0.25, ((1, 8),))
    w_uv = centred(streams_of[5], (LAT, HEADS * VDIM), LAT ** -0.5, 0.25, ((1, 8),))
    segment_ids = jax.vmap(lambda own: jnp.searchsorted(jnp.cumsum(uneven(own, SEGS, SEQ, SEQ // 2, 1)), jnp.arange(SEQ), side="right"))(jax.random.split(streams_of[6], ROLLOUTS)).reshape((ROLLOUTS, SEQ)).astype(jnp.int32)
    span_order = draw_span_order(jax.random.fold_in(streams_of[8], 71), 0)
    return {"q_nope": q_nope, "q_rope": q_rope, "kv_latent": kv_latent, "d_out": d_out, "w_uk": w_uk, "w_uv": w_uv, "segment_ids": segment_ids, "span_order": span_order}


def storage_positions(span_order, seq_rows):
    span_rows = seq_rows // span_order.shape[0]
    slot_ids = jnp.arange(seq_rows, dtype=jnp.int32)
    numbers = jnp.arange(span_order.shape[0], dtype=jnp.int32)
    owners = jnp.sum(jnp.where((slot_ids // span_rows)[:, None] == numbers[None, :], span_order[None, :], 0), axis=1)
    return (owners * span_rows + slot_ids % span_rows).astype(jnp.int32)


def rollout_grads(nope_rows, rope_rows, latents, cotangent, uk_heads, uv_heads, seg_seq, span_order):
    places = storage_positions(span_order, SEQ)
    labels = jnp.take(seg_seq, places)
    visible = (labels[:, None] == labels[None, :]) & (places[None, :] <= places[:, None])
    softmax_scale = (NOPE + ROPE) ** -0.5
    content = latents[:, :LAT]
    nope_heads = nope_rows.reshape(SEQ, HEADS, NOPE).transpose(1, 0, 2)
    rope_heads = rope_rows.reshape(SEQ, HEADS, ROPE).transpose(1, 0, 2)
    grad_heads = cotangent.reshape(SEQ, HEADS, VDIM).transpose(1, 0, 2)

    def per_head(latent_grad, pieces):
        q_part, r_part, g_part, uk_part, uv_part = pieces
        q_latent = jnp.dot(q_part, uk_part.T, preferred_element_type=jnp.float32).astype(jnp.bfloat16)
        q_full = jnp.concatenate([q_latent, r_part], axis=1)
        scores = jnp.dot(q_full, latents.T, preferred_element_type=jnp.float32) * softmax_scale
        row_max = jnp.max(jnp.where(visible, scores, -1e30), axis=1)
        row_sum = jnp.sum(jnp.where(visible, jnp.exp(scores - row_max[:, None]), 0.0), axis=1)
        lse = row_max + jnp.log(row_sum)
        probs = jnp.where(visible, jnp.exp(scores - lse[:, None]), 0.0)
        probs_bf = probs.astype(jnp.bfloat16)
        o_latent = jnp.dot(probs_bf, content, preferred_element_type=jnp.float32)
        do_latent = jnp.dot(g_part, uv_part.T, preferred_element_type=jnp.float32)
        do_bf = do_latent.astype(jnp.bfloat16)
        row_dot = jnp.sum(do_latent * o_latent, axis=1)
        dprobs = jnp.dot(do_bf, content.T, preferred_element_type=jnp.float32)
        dscores = (probs * (dprobs - row_dot[:, None]) * softmax_scale).astype(jnp.bfloat16)
        dq_full = jnp.dot(dscores, latents, preferred_element_type=jnp.float32)
        dq_latent = dq_full[:, :LAT].astype(jnp.bfloat16)
        dq_nope = jnp.dot(dq_latent, uk_part, preferred_element_type=jnp.float32).astype(jnp.bfloat16)
        dq_rope = dq_full[:, LAT:].astype(jnp.bfloat16)
        value_part = jnp.dot(probs_bf.T, do_bf, preferred_element_type=jnp.float32)
        kv_term = jnp.dot(dscores.T, q_full, preferred_element_type=jnp.float32)
        kv_term = kv_term + jnp.concatenate([value_part, jnp.zeros((SEQ, ROPE), jnp.float32)], axis=1)
        uk_grad = jnp.dot(dq_latent.T, q_part, preferred_element_type=jnp.float32)
        uv_grad = jnp.dot(o_latent.astype(jnp.bfloat16).T, g_part, preferred_element_type=jnp.float32)
        return latent_grad + kv_term, (dq_nope, dq_rope, uk_grad, uv_grad)

    zero_grad = jnp.zeros((SEQ, LAT + ROPE), jnp.float32)
    return lax.scan(per_head, zero_grad, (nope_heads, rope_heads, grad_heads, uk_heads, uv_heads))


def reference(q_nope, q_rope, kv_latent, d_out, w_uk, w_uv, segment_ids, span_order):
    uk_heads = w_uk.reshape(LAT, HEADS, NOPE).transpose(1, 0, 2)
    uv_heads = w_uv.reshape(LAT, HEADS, VDIM).transpose(1, 0, 2)
    nope_out = []
    rope_out = []
    latent_out = []
    uk_total = jnp.zeros((HEADS, LAT, NOPE), jnp.float32)
    uv_total = jnp.zeros((HEADS, LAT, VDIM), jnp.float32)
    for rollout in range(ROLLOUTS):
        latent_grad, stacked = rollout_grads(q_nope[rollout], q_rope[rollout], kv_latent[rollout], d_out[rollout], uk_heads, uv_heads, segment_ids[rollout], span_order)
        head_nope, head_rope, uk_grad, uv_grad = stacked
        nope_out.append(head_nope.transpose(1, 0, 2).reshape(SEQ, HEADS * NOPE))
        rope_out.append(head_rope.transpose(1, 0, 2).reshape(SEQ, HEADS * ROPE))
        latent_out.append(latent_grad.astype(jnp.bfloat16))
        uk_total = uk_total + uk_grad
        uv_total = uv_total + uv_grad
    dw_uk = uk_total.transpose(1, 0, 2).reshape(LAT, HEADS * NOPE)
    dw_uv = uv_total.transpose(1, 0, 2).reshape(LAT, HEADS * VDIM)
    return (jnp.stack(nope_out), jnp.stack(rope_out), jnp.stack(latent_out), dw_uk, dw_uv)
```

```python
import jax
import jax.numpy as jnp
from jax import lax
from jax.experimental import pallas as pl
from jax.experimental.pallas import tpu as pltpu
from jax.sharding import Mesh, PartitionSpec as P

LAT = 512
ROPE = 64
NOPE = 128
VDIM = 128
SEQ = 1024
SPAN = 64
SCALE = (NOPE + ROPE) ** -0.5
F32 = jnp.float32
BF16 = jnp.bfloat16
MIB = 1 << 20


def dot(a, b, dims):
    return lax.dot_general(a, b, (dims, ((), ())), preferred_element_type=F32)


NN = ((1,), (0,))
NT = ((1,), (1,))
TN = ((0,), (0,))


def pack_kernel(qn_ref, qr_ref, do_ref, kv_ref, x_ref, k_ref):
    for h in range(8):
        x_ref[h, 0:128, :] = qn_ref[0, :, h * 128:(h + 1) * 128]
        x_ref[h, 128:256, :] = do_ref[0, :, h * 128:(h + 1) * 128]
        x_ref[h, 256:320, 0:64] = qr_ref[0, 0:64, h * 64:(h + 1) * 64]
        x_ref[h, 256:320, 64:128] = qr_ref[0, 64:128, h * 64:(h + 1) * 64]
    for j in range(4):
        k_ref[j * 128:(j + 1) * 128, :] = kv_ref[0, :, j * 128:(j + 1) * 128]
    k_ref[512:576, 0:64] = kv_ref[0, 0:64, 512:576]
    k_ref[512:576, 64:128] = kv_ref[0, 64:128, 512:576]


def pack(q_nope, q_rope, d_out, kv):
    return pl.pallas_call(
        pack_kernel,
        out_shape=(
            jax.ShapeDtypeStruct((8, 320, 128), BF16),
            jax.ShapeDtypeStruct((576, 128), BF16),
        ),
        compiler_params=pltpu.CompilerParams(vmem_limit_bytes=16 * MIB),
        name="pack",
    )(q_nope, q_rope, d_out, kv)


def main_kernel(order_ref, ids_ref, x_ref, *refs):
    kv_refs = refs[:8]
    uk_ref, uv_ref, segc_ref, segr_ref = refs[8:12]
    dq_ref, keep_ref, send_ref, dw_ref = refs[12:16]
    keys, qfull, qn, g, dob, dkv, dqs, dwk, dwv = refs[16:]
    y = ids_ref[0]
    core = ids_ref[1]

    for slot in range(16):
        c, e = slot // 2, slot % 2
        row = pl.ds(pl.multiple_of(order_ref[slot] * SPAN, SPAN), SPAN)
        qn[row, :] = x_ref[c, e * 64:(e + 1) * 64, :]
        g[row, :] = x_ref[c, 128 + e * 64:128 + (e + 1) * 64, :]
        qfull[row, LAT:LAT + ROPE] = x_ref[c, 256:320, e * 64:(e + 1) * 64]
    for d in range(4):
        for cr in range(2):
            ref = kv_refs[d * 2 + cr]
            ctx = (y ^ d) * 2 + (core ^ cr)
            for e in range(2):
                row = pl.ds(pl.multiple_of(order_ref[ctx * 2 + e] * SPAN, SPAN), SPAN)
                for j in range(4):
                    keys[row, j * 128:(j + 1) * 128] = ref[j * 128 + e * 64:j * 128 + (e + 1) * 64, :]
                keys[row, LAT:LAT + ROPE] = ref[512:576, e * 64:(e + 1) * 64]
    uk = uk_ref[...]
    uv = uv_ref[...]
    qfull[:, 0:LAT] = dot(qn[...], uk, NT).astype(BF16)
    dob[...] = dot(g[...], uv, NT).astype(BF16)
    dkv[...] = jnp.zeros_like(dkv)
    dwk[...] = jnp.zeros_like(dwk)
    dwv[...] = jnp.zeros_like(dwv)

    for b in range(4):
        q0 = b * 256
        w0 = max(0, q0 - 512)
        w1 = q0 + 256
        width = w1 - w0
        kw = keys[w0:w1, :]
        qb = qfull[q0:w1, :]
        do_b = dob[q0:w1, :]
        scores = dot(qb, kw, NT) * SCALE
        rows = lax.broadcasted_iota(jnp.int32, (256, width), 0) + q0
        cols = lax.broadcasted_iota(jnp.int32, (256, width), 1) + w0
        visible = (segc_ref[q0:w1, :] == segr_ref[:, w0:w1]) & (cols <= rows)
        scores = jnp.where(visible, scores, -1e30)
        top = jnp.max(scores, axis=1, keepdims=True)
        ex = jnp.exp(scores - top)
        probs = ex * (1.0 / jnp.sum(ex, axis=1, keepdims=True))
        pb = probs.astype(BF16)
        o_lat = dot(pb, kw[:, 0:LAT], NN)
        dprobs = dot(do_b, kw[:, 0:LAT], NT)
        row_dot = jnp.sum(probs * dprobs, axis=1, keepdims=True)
        ds = (probs * (dprobs - row_dot) * SCALE).astype(BF16)
        dq = dot(ds, kw, NN)
        dkv[w0:w1, :] += dot(ds, qb, TN)
        dkv[w0:w1, 0:LAT] += dot(pb, do_b, TN)
        dql = dq[:, 0:LAT].astype(BF16)
        dqs[q0:w1, 0:128] = dot(dql, uk, NN).astype(BF16)
        dqs[q0:w1, 128:192] = dq[:, LAT:].astype(BF16)
        dwk[...] += dot(dql, qn[q0:w1, :], TN)
        dwv[...] += dot(o_lat.astype(BF16), g[q0:w1, :], TN)

    dw_ref[0:512, :] = dwk[...].astype(BF16)
    dw_ref[512:1024, :] = dwv[...].astype(BF16)
    for slot in range(16):
        c, e = slot // 2, slot % 2
        row = pl.ds(pl.multiple_of(order_ref[slot] * SPAN, SPAN), SPAN)
        dq_ref[c, e * 64:(e + 1) * 64, :] = dqs[row, 0:128]
        dq_ref[c, 128:192, e * 64:(e + 1) * 64] = dqs[row, 128:192]
        part = dkv[row, :].astype(BF16)
        out_row = pl.ds((c // 2) * 128 + e * 64, 64)

        @pl.when(core == c % 2)
        def _():
            keep_ref[out_row, :] = part

        @pl.when(core != c % 2)
        def _():
            send_ref[out_row, :] = part


def attend(order, ids, x, kvs, w_uk, w_uv, segc, segr):
    def full(shape):
        return pl.BlockSpec(shape, lambda i, order, ids: (0,) * len(shape))

    head = pl.BlockSpec((LAT, 128), lambda i, order, ids: (0, ids[0] * 2 + ids[1]))
    return pl.pallas_call(
        main_kernel,
        grid_spec=pltpu.PrefetchScalarGridSpec(
            num_scalar_prefetch=2,
            grid=(1,),
            in_specs=[full((8, 320, 128))] + [full((576, 128))] * 8
            + [head, head, full((SEQ, 1)), full((1, SEQ))],
            out_specs=[full((8, 192, 128)), full((512, 576)), full((512, 576)), full((1024, 128))],
            scratch_shapes=[
                pltpu.VMEM((SEQ, 576), BF16),
                pltpu.VMEM((SEQ, 576), BF16),
                pltpu.VMEM((SEQ, 128), BF16),
                pltpu.VMEM((SEQ, 128), BF16),
                pltpu.VMEM((SEQ, LAT), BF16),
                pltpu.VMEM((SEQ, 576), F32),
                pltpu.VMEM((SEQ, 192), BF16),
                pltpu.VMEM((LAT, 128), F32),
                pltpu.VMEM((LAT, 128), F32),
            ],
        ),
        out_shape=(
            jax.ShapeDtypeStruct((8, 192, 128), BF16),
            jax.ShapeDtypeStruct((512, 576), BF16),
            jax.ShapeDtypeStruct((512, 576), BF16),
            jax.ShapeDtypeStruct((1024, 128), BF16),
        ),
        compiler_params=pltpu.CompilerParams(vmem_limit_bytes=48 * MIB),
        name="attend",
    )(order, ids, x, *kvs, w_uk, w_uv, segc, segr)


def unpack_kernel(x_ref, qn_ref, qr_ref):
    for h in range(8):
        qn_ref[0, :, h * 128:(h + 1) * 128] = x_ref[h, 0:128, :]
        qr_ref[0, 0:64, h * 64:(h + 1) * 64] = x_ref[h, 128:192, 0:64]
        qr_ref[0, 64:128, h * 64:(h + 1) * 64] = x_ref[h, 128:192, 64:128]


def unpack(x):
    return pl.pallas_call(
        unpack_kernel,
        out_shape=(
            jax.ShapeDtypeStruct((1, 128, 1024), BF16),
            jax.ShapeDtypeStruct((1, 128, 512), BF16),
        ),
        compiler_params=pltpu.CompilerParams(vmem_limit_bytes=16 * MIB),
        name="unpack",
    )(x)


def widen_kernel(ids_ref, mine_ref, sib_ref, uk_ref, uv_ref):
    core = ids_ref[1]
    at = pl.ds(pl.multiple_of(core * 128, 128), 128)
    other = pl.ds(pl.multiple_of((1 - core) * 128, 128), 128)
    uk_ref[:, at] = mine_ref[0, 0:512, :].astype(F32)
    uk_ref[:, other] = sib_ref[0, 0:512, :].astype(F32)
    uv_ref[:, at] = mine_ref[0, 512:1024, :].astype(F32)
    uv_ref[:, other] = sib_ref[0, 512:1024, :].astype(F32)


def widen(ids, mine, sib):
    piece = pl.BlockSpec((1, 1024, 128), lambda i, ids: (i, 0, 0))
    out = pl.BlockSpec((512, 256), lambda i, ids: (0, i))
    return pl.pallas_call(
        widen_kernel,
        grid_spec=pltpu.PrefetchScalarGridSpec(
            num_scalar_prefetch=1, grid=(4,), in_specs=[piece, piece], out_specs=[out, out]
        ),
        out_shape=(jax.ShapeDtypeStruct((512, 1024), F32),) * 2,
        compiler_params=pltpu.CompilerParams(vmem_limit_bytes=16 * MIB),
        name="widen",
    )(ids, mine, sib)


def across(x, axis, step):
    size = 2 if axis == "core" else 4
    return lax.ppermute(x, axis, [(i, i ^ step) for i in range(size)])


def local(q_nope, q_rope, kv_latent, d_out, w_uk, w_uv, segment_ids, span_order):
    y = lax.axis_index("y")
    core = lax.axis_index("core")
    ids = jnp.stack([y, core]).astype(jnp.int32)
    send, kvp = pack(q_nope, q_rope, d_out, kv_latent)
    col = [kvp] + [across(kvp, "y", d) for d in (1, 2, 3)]
    x = lax.all_to_all(send, ("y", "core"), 0, 0, tiled=True)
    kvs = []
    for piece in col:
        kvs += [piece, across(piece, "core", 1)]
    dq, keep, away, dw = attend(
        span_order, ids, x, kvs, w_uk, w_uv, segment_ids.reshape(SEQ, 1), segment_ids
    )
    came = across(away, "core", 1)
    half = (keep.astype(F32) + came.astype(F32)).astype(BF16).reshape(32, 16, 576)
    parts = lax.all_to_all(half, ("y", "zl", "x"), 0, 0, tiled=True)
    d_kv = jnp.sum(parts.astype(F32), axis=0).astype(BF16)[None]
    pieces = lax.all_to_all(dw.reshape(4, 256, 128), "dp", 0, 0, tiled=True)
    total = jnp.sum(pieces.astype(F32), axis=0).astype(BF16)
    whole = lax.all_to_all(jnp.broadcast_to(total[None], (4, 256, 128)), "dp", 0, 0, tiled=True)
    whole = whole.reshape(1, 1024, 128)
    mine = lax.all_to_all(jnp.broadcast_to(whole, (4, 1024, 128)), "y", 0, 0, tiled=True)
    sib = across(mine, "core", 1)
    dw_uk, dw_uv = widen(ids, mine, sib)
    back = lax.all_to_all(dq, ("y", "core"), 0, 0, tiled=True)
    dq_nope, dq_rope = unpack(back)
    return dq_nope, dq_rope, d_kv, dw_uk, dw_uv


def solution(mesh):
    split = Mesh(mesh.devices.reshape(4, 4, 2, 2, 4), ("dp", "y", "core", "zl", "x"))
    ctx = ("y", "core")
    head = ("zl", "x")
    return jax.shard_map(
        local,
        mesh=split,
        in_specs=(
            P("dp", ctx, head),
            P("dp", ctx, head),
            P("dp", ctx, None),
            P("dp", ctx, head),
            P(None, head),
            P(None, head),
            P("dp", None),
            P(),
        ),
        out_specs=(
            P("dp", ctx, head),
            P("dp", ctx, head),
            P("dp", ctx + head, None),
            P(None, head),
            P(None, head),
        ),
        check_vma=False,
    )
```

```python
import jax
import jax.numpy as jnp
from jax import lax
from jax.experimental import pallas as pl
from jax.experimental.pallas import tpu as pltpu
from jax.sharding import Mesh, PartitionSpec as P

LAT = 512
ROPE = 64
NOPE = 128
VDIM = 128
SEQ = 1024
SPAN = 64
SCALE = (NOPE + ROPE) ** -0.5
F32 = jnp.float32
BF16 = jnp.bfloat16
MIB = 1 << 20
LOG2E = 1.4426950408889634


def dot(a, b, dims):
    return lax.dot_general(a, b, (dims, ((), ())), preferred_element_type=F32)


NN = ((1,), (0,))
NT = ((1,), (1,))
TN = ((0,), (0,))


def pack_kernel(qn_ref, qr_ref, do_ref, after_ref, x_ref):
    for h in range(8):
        x_ref[h, 0:128, :] = qn_ref[0, :, h * 128:(h + 1) * 128]
        x_ref[h, 128:256, :] = do_ref[0, :, h * 128:(h + 1) * 128]
        x_ref[h, 256:320, 0:64] = qr_ref[0, 0:64, h * 64:(h + 1) * 64]
        x_ref[h, 256:320, 64:128] = qr_ref[0, 64:128, h * 64:(h + 1) * 64]


def pack(q_nope, q_rope, d_out, after):
    whole = pl.BlockSpec(memory_space=pltpu.VMEM)
    return pl.pallas_call(
        pack_kernel,
        in_specs=[whole] * 3 + [pl.BlockSpec(memory_space=pl.ANY)],
        out_specs=whole,
        out_shape=jax.ShapeDtypeStruct((8, 320, 128), BF16),
        compiler_params=pltpu.CompilerParams(vmem_limit_bytes=60 * MIB),
        cost_estimate=pl.CostEstimate(flops=0, bytes_accessed=5 * MIB, transcendentals=0),
        name="pack",
    )(q_nope, q_rope, d_out, after)


def attend_kernel(order_ref, x_hbm, *refs):
    kv_hbm = refs[:8]
    uk_hbm, uv_hbm, seg_ref = refs[8:11]
    back_ref = refs[11]
    dw_refs = refs[12:16]
    x_in, kv_in, uk_in, uv_in, keys, keyt, qfull, qn, g, dob, pt, dst, ot, dqt, dqr, dqs, dkv, dw, sems = refs[16:]
    y = lax.axis_index("y")
    core = lax.axis_index("core")
    me = y * 2 + core
    block = y ^ lax.axis_index("x")
    cols = pl.ds(pl.multiple_of(me * 128, 128), 128)

    load_x = pltpu.make_async_copy(x_hbm, x_in, sems.at[8])
    load_uk = pltpu.make_async_copy(uk_hbm.at[:, cols], uk_in, sems.at[9])
    load_uv = pltpu.make_async_copy(uv_hbm.at[:, cols], uv_in, sems.at[10])
    loads = [pltpu.make_async_copy(kv_hbm[i], kv_in.at[i], sems.at[i]) for i in range(8)]
    for load in [load_x, load_uk, load_uv] + loads:
        load.start()

    load_x.wait()
    for slot in range(16):
        c, e = slot // 2, slot % 2
        row = pl.ds(pl.multiple_of(order_ref[slot] * SPAN, SPAN), SPAN)
        qn[row, :] = x_in[c, e * 64:(e + 1) * 64, :]
        g[row, :] = x_in[c, 128 + e * 64:128 + (e + 1) * 64, :]
        qfull[row, LAT:LAT + ROPE] = x_in[c, 256:320, e * 64:(e + 1) * 64]
    load_uk.wait()
    load_uv.wait()
    uk = uk_in[...]
    qfull[:, 0:LAT] = dot(qn[...], uk, NT).astype(BF16)
    dob[...] = dot(g[...], uv_in[...], NT).astype(BF16)
    for d in range(4):
        for cr in range(2):
            i = d * 2 + cr
            ctx = (block ^ d) * 2 + (core ^ cr)
            loads[i].wait()
            piece = jnp.transpose(kv_in[i], (1, 0))
            for e in range(2):
                row = pl.ds(pl.multiple_of(order_ref[ctx * 2 + e] * SPAN, SPAN), SPAN)
                keys[row, :] = piece[e * 64:(e + 1) * 64, :]
    for b in range(4):
        keyt[:, b * 256:(b + 1) * 256] = jnp.transpose(keys[b * 256:(b + 1) * 256, :], (1, 0))
    seg = seg_ref[...]
    begin = jnp.zeros_like(seg)
    for v in range(1, 4):
        below = jnp.sum((seg < v).astype(jnp.int32), axis=1, keepdims=True)
        begin = jnp.where(seg >= v, below, begin)

    def window(b):
        return max(0, b * 256 - 512), b * 256, b * 256 + 256

    def products(b):
        w0, q0, w1 = window(b)
        kw = keys[w0:w1, :]
        return dot(kw, qfull[q0:w1, :], NT), dot(kw[:, 0:LAT], dob[q0:w1, :], NT)

    def softmax(b, scores, dprobs):
        w0, q0, w1 = window(b)
        width = w1 - w0
        k_at = lax.broadcasted_iota(jnp.int32, (width, 256), 0) + w0
        q_at = lax.broadcasted_iota(jnp.int32, (1, 256), 1) + q0
        visible = (k_at >= begin[:, q0:w1]) & (k_at <= q_at)
        scores = jnp.where(visible, scores, -1e30)
        top = jnp.max(scores, axis=0, keepdims=True)
        ex = jnp.exp2((scores - top) * (SCALE * LOG2E))
        probs = ex * (1.0 / jnp.sum(ex, axis=0, keepdims=True))
        row_dot = jnp.sum(probs * dprobs, axis=0, keepdims=True)
        pb = probs.astype(BF16)
        ds = ((probs * SCALE) * (dprobs - row_dot)).astype(BF16)
        pt[b, 0:width, :] = pb
        dst[b, 0:width, :] = ds

    def outputs(b):
        w0, q0, w1 = window(b)
        width = w1 - w0
        ot[:, q0:w1] = dot(keyt[0:LAT, w0:w1], pt[b, 0:width, :], NN).astype(BF16)
        dq = dot(keyt[:, w0:w1], dst[b, 0:width, :], NN)
        dqt[:, q0:w1] = dq[0:LAT, :].astype(BF16)
        dqr[:, q0:w1] = dq[LAT:, :].astype(BF16)

    flight = products(0)
    for b in range(4):
        following = products(b + 1) if b < 3 else None
        softmax(b, *flight)
        outputs(b)
        flight = following
    dw[0:512, :] = dot(dqt[...], qn[...], NN).astype(BF16)
    dw[512:1024, :] = dot(ot[...], g[...], NN).astype(BF16)
    dp = lax.axis_index("dp")
    for d in range(4):
        dw_refs[d][...] = dw[pl.ds(pl.multiple_of((dp ^ d) * 256, 256), 256), :]
    dqs[:, 0:128] = dot(dqt[...], uk, TN).astype(BF16)
    dqs[:, 128:192] = jnp.transpose(dqr[...], (1, 0))
    for slot in range(16):
        c, e = slot // 2, slot % 2
        row = pl.ds(pl.multiple_of(order_ref[slot] * SPAN, SPAN), SPAN)
        back_ref[c, 576 + e * 64:576 + (e + 1) * 64, :] = dqs[row, 0:128]
        back_ref[c, 704:768, e * 64:(e + 1) * 64] = dqs[row, 128:192]

    for kb in range(4):
        last = min(kb + 3, 4)
        ds = []
        pb = []
        for b in range(kb, last):
            at = kb * 256 - max(0, b * 256 - 512)
            ds.append(dst[b, at:at + 256, :])
            pb.append(pt[b, at:at + 256, :])
        ds = jnp.concatenate(ds, axis=1)
        pb = jnp.concatenate(pb, axis=1)
        lo, hi = kb * 256, last * 256
        dkv[lo:lo + 256, 0:LAT] = (dot(ds, qfull[lo:hi, 0:LAT], NN) + dot(pb, dob[lo:hi, :], NN)).astype(BF16)
        dkv[lo:lo + 256, LAT:] = dot(ds, qfull[lo:hi, LAT:], NN).astype(BF16)
    for slot in range(16):
        c, e = slot // 2, slot % 2
        row = pl.ds(pl.multiple_of(order_ref[slot] * SPAN, SPAN), SPAN)
        for j in range(4):
            back_ref[c, j * 128 + e * 64:j * 128 + (e + 1) * 64, :] = dkv[row, j * 128:(j + 1) * 128]
        back_ref[c, 512:576, e * 64:(e + 1) * 64] = dkv[row, LAT:LAT + ROPE]


def attend(order, x, kvs, w_uk, w_uv, seg):
    hbm = pl.BlockSpec(memory_space=pl.ANY)
    vmem = pl.BlockSpec(memory_space=pltpu.VMEM)
    outs = [(8, 768, 128)] + [(256, 128)] * 4
    return pl.pallas_call(
        attend_kernel,
        in_specs=[pl.BlockSpec(memory_space=pltpu.SMEM)] + [hbm] * 11 + [vmem],
        out_specs=[vmem] * 5,
        scratch_shapes=[
            pltpu.VMEM((8, 320, 128), BF16),
            pltpu.VMEM((8, 576, 128), BF16),
            pltpu.VMEM((LAT, 128), BF16),
            pltpu.VMEM((LAT, 128), BF16),
            pltpu.VMEM((SEQ, 576), BF16),
            pltpu.VMEM((576, SEQ), BF16),
            pltpu.VMEM((SEQ, 576), BF16),
            pltpu.VMEM((SEQ, 128), BF16),
            pltpu.VMEM((SEQ, 128), BF16),
            pltpu.VMEM((SEQ, LAT), BF16),
            pltpu.VMEM((4, 768, 256), BF16),
            pltpu.VMEM((4, 768, 256), BF16),
            pltpu.VMEM((LAT, SEQ), BF16),
            pltpu.VMEM((LAT, SEQ), BF16),
            pltpu.VMEM((64, SEQ), BF16),
            pltpu.VMEM((SEQ, 192), BF16),
            pltpu.VMEM((SEQ, 576), BF16),
            pltpu.VMEM((1024, 128), BF16),
            pltpu.SemaphoreType.DMA((11,)),
        ],
        out_shape=[jax.ShapeDtypeStruct(shape, BF16) for shape in outs],
        compiler_params=pltpu.CompilerParams(vmem_limit_bytes=60 * MIB),
        cost_estimate=pl.CostEstimate(flops=9_000_000_000, bytes_accessed=12 * MIB, transcendentals=600_000),
        name="attend",
    )(order, x, *kvs, w_uk, w_uv, seg)


def call(kernel, name, out, *args):
    return pl.pallas_call(
        kernel,
        out_shape=out,
        compiler_params=pltpu.CompilerParams(vmem_limit_bytes=16 * MIB),
        cost_estimate=pl.CostEstimate(flops=0, bytes_accessed=3 * MIB, transcendentals=0),
        name=name,
    )(*args)


def sum4_kernel(a_ref, b_ref, c_ref, d_ref, out_ref):
    total = (a_ref[...].astype(F32) + b_ref[...].astype(F32)) + (c_ref[...].astype(F32) + d_ref[...].astype(F32))
    out_ref[...] = total.astype(BF16)


def sum_ctx_kernel(x_ref, out_ref):
    total = x_ref[0].astype(F32)
    for i in range(1, 8):
        total = total + x_ref[i].astype(F32)
    total = total.astype(BF16)
    for i in range(8):
        for j in range(4):
            out_ref[i, :, j * 128:(j + 1) * 128] = total[j * 128 + i * 16:j * 128 + (i + 1) * 16, :]
        lane = (i // 4) * 64
        low = 512 + (i % 4) * 16
        out_ref[i, :, 512:576] = total[low:low + 16, lane:lane + 64]
        out_ref[i, :, 576:640] = jnp.zeros((16, 64), BF16)


def sum_ctx(x):
    return pl.pallas_call(
        sum_ctx_kernel,
        grid=(1,),
        in_specs=[pl.BlockSpec((8, 576, 128), lambda i: (0, 0, 0))],
        out_specs=pl.BlockSpec((8, 16, 640), lambda i: (0, 0, 0)),
        out_shape=jax.ShapeDtypeStruct((8, 16, 640), BF16),
        compiler_params=pltpu.CompilerParams(vmem_limit_bytes=16 * MIB),
        name="sum_ctx",
    )(x)


def sum_head_kernel(x_ref, out_ref):
    total = x_ref[0].astype(F32)
    for i in range(1, 8):
        total = total + x_ref[i].astype(F32)
    out_ref[0] = total[:, 0:576].astype(BF16)


def join_kernel(a_ref, b_ref, c_ref, d_ref, out_ref):
    dp = lax.axis_index("dp")
    for d, ref in enumerate((a_ref, b_ref, c_ref, d_ref)):
        out_ref[pl.ds(pl.multiple_of((dp ^ d) * 256, 256), 256), :] = ref[...]


def unpack_kernel(x_ref, qn_ref, qr_ref):
    for h in range(8):
        qn_ref[0, :, h * 128:(h + 1) * 128] = x_ref[h, 0:128, :]
        qr_ref[0, 0:64, h * 64:(h + 1) * 64] = x_ref[h, 128:192, 0:64]
        qr_ref[0, 64:128, h * 64:(h + 1) * 64] = x_ref[h, 128:192, 64:128]


def unpack(x):
    return pl.pallas_call(
        unpack_kernel,
        grid=(1,),
        in_specs=[pl.BlockSpec((8, 192, 128), lambda i: (0, 3, 0))],
        out_specs=[
            pl.BlockSpec((1, 128, 1024), lambda i: (0, 0, 0)),
            pl.BlockSpec((1, 128, 512), lambda i: (0, 0, 0)),
        ],
        out_shape=(
            jax.ShapeDtypeStruct((1, 128, 1024), BF16),
            jax.ShapeDtypeStruct((1, 128, 512), BF16),
        ),
        compiler_params=pltpu.CompilerParams(vmem_limit_bytes=16 * MIB),
        name="unpack",
    )(x)


def widen_kernel(*refs):
    uk_ref, uv_ref = refs[8:]
    y = lax.axis_index("y")
    core = lax.axis_index("core")
    for d in range(4):

        @pl.when(pl.program_id(0) == (y ^ d))
        def _():
            for cr in range(2):
                ref = refs[d * 2 + cr]
                at = pl.ds(pl.multiple_of((core ^ cr) * 128, 128), 128)
                uk_ref[:, at] = ref[0:512, :].astype(F32)
                uv_ref[:, at] = ref[512:1024, :].astype(F32)


def widen(pieces):
    piece = pl.BlockSpec((1024, 128), lambda i: (0, 0))
    out = pl.BlockSpec((512, 256), lambda i: (0, i))
    return pl.pallas_call(
        widen_kernel,
        grid=(4,),
        in_specs=[piece] * 8,
        out_specs=[out, out],
        out_shape=(jax.ShapeDtypeStruct((512, 1024), F32),) * 2,
        compiler_params=pltpu.CompilerParams(vmem_limit_bytes=16 * MIB),
        name="widen",
    )(*pieces)


SIZES = {"core": 2, "x": 4, "y": 4, "dp": 4}


def across(x, axis, step):
    return lax.ppermute(x, axis, [(i, i ^ step) for i in range(SIZES[axis])])


def local(q_nope, q_rope, kv_latent, d_out, w_uk, w_uv, segment_ids, span_order):
    kvt = kv_latent[0].T
    skew = [(i * 4 + j, (i ^ j) * 4 + j) for i in range(4) for j in range(4)]
    first = lax.ppermute(kvt, ("y", "x"), skew)
    kvs = []
    for piece in [first] + [across(first, "x", d) for d in (1, 2, 3)]:
        kvs += [piece, across(piece, "core", 1)]
    send = pack(q_nope, q_rope, d_out, kvt)
    send, first = lax.optimization_barrier((send, first))
    x = lax.all_to_all(send, ("y", "core"), 0, 0, tiled=True)
    back, dw0, dw1, dw2, dw3 = attend(span_order, x, kvs, w_uk, w_uv, segment_ids)
    back = lax.all_to_all(back, ("y", "core"), 0, 0, tiled=True)
    dq_nope, dq_rope = unpack(back)
    parts = lax.all_to_all(sum_ctx(back), ("zl", "x"), 0, 0, tiled=True)
    d_kv = call(sum_head_kernel, "sum_head", jax.ShapeDtypeStruct((1, 16, 576), BF16), parts)
    chunk = jax.ShapeDtypeStruct((256, 128), BF16)
    total = call(sum4_kernel, "sum4", chunk, dw0, across(dw1, "dp", 1), across(dw2, "dp", 2), across(dw3, "dp", 3))
    gathered = [across(total, "dp", d) for d in (1, 2, 3)]
    whole = call(join_kernel, "join", jax.ShapeDtypeStruct((1024, 128), BF16), total, *gathered)
    pieces = []
    for piece in [whole] + [across(whole, "y", d) for d in (1, 2, 3)]:
        pieces += [piece, across(piece, "core", 1)]
    dw_uk, dw_uv = widen(pieces)
    return dq_nope, dq_rope, d_kv, dw_uk, dw_uv


def solution(mesh):
    split = Mesh(mesh.devices.reshape(4, 4, 2, 2, 4), ("dp", "y", "core", "zl", "x"))
    ctx = ("y", "core")
    head = ("zl", "x")
    return jax.shard_map(
        local,
        mesh=split,
        in_specs=(
            P("dp", ctx, head),
            P("dp", ctx, head),
            P("dp", ctx, None),
            P("dp", ctx, head),
            P(None, head),
            P(None, head),
            P("dp", None),
            P(),
        ),
        out_specs=(
            P("dp", ctx, head),
            P("dp", ctx, head),
            P("dp", ctx + head, None),
            P(None, head),
            P(None, head),
        ),
        check_vma=False,
    )
```

```python
import jax
import jax.numpy as jnp
from jax import lax
from jax.experimental import pallas as pl
from jax.experimental.pallas import tpu as pltpu
from jax.sharding import Mesh, PartitionSpec as P

LAT = 512
ROPE = 64
NOPE = 128
VDIM = 128
SEQ = 1024
SPAN = 64
SCALE = (NOPE + ROPE) ** -0.5
F32 = jnp.float32
BF16 = jnp.bfloat16
MIB = 1 << 20
LOG2E = 1.4426950408889634


def dot(a, b, dims):
    return lax.dot_general(a, b, (dims, ((), ())), preferred_element_type=F32)


NN = ((1,), (0,))
NT = ((1,), (1,))
TN = ((0,), (0,))


def pack_kernel(qn_ref, qr_ref, do_ref, after_ref, x_ref):
    for h in range(8):
        x_ref[h, 0:128, :] = qn_ref[0, :, h * 128:(h + 1) * 128]
        x_ref[h, 128:256, :] = do_ref[0, :, h * 128:(h + 1) * 128]
        x_ref[h, 256:320, 0:64] = qr_ref[0, 0:64, h * 64:(h + 1) * 64]
        x_ref[h, 256:320, 64:128] = qr_ref[0, 64:128, h * 64:(h + 1) * 64]


def pack(q_nope, q_rope, d_out, after):
    whole = pl.BlockSpec(memory_space=pltpu.VMEM)
    return pl.pallas_call(
        pack_kernel,
        in_specs=[whole] * 3 + [pl.BlockSpec(memory_space=pl.ANY)],
        out_specs=whole,
        out_shape=jax.ShapeDtypeStruct((8, 320, 128), BF16),
        compiler_params=pltpu.CompilerParams(vmem_limit_bytes=60 * MIB),
        cost_estimate=pl.CostEstimate(flops=0, bytes_accessed=5 * MIB, transcendentals=0),
        name="pack",
    )(q_nope, q_rope, d_out, after)


def attend_kernel(order_ref, x_in, *refs):
    kv_hbm = refs[:8]
    uk_hbm, uv_hbm, seg_ref = refs[8:11]
    back_ref = refs[11]
    duk_ref, duv_ref = refs[12:14]
    kv_in, uk_in, uv_in, keys, keyt, qfull, qn, g, dob, pt, dst, ot, dqt, dqr, dqs, dkr, inverse, sems = refs[14:]
    y = lax.axis_index("y")
    core = lax.axis_index("core")
    me = y * 2 + core
    block = y ^ lax.axis_index("x")
    cols = pl.ds(pl.multiple_of(me * 128, 128), 128)

    load_uk = pltpu.make_async_copy(uk_hbm.at[:, cols], uk_in, sems.at[9])
    load_uv = pltpu.make_async_copy(uv_hbm.at[:, cols], uv_in, sems.at[10])
    loads = [pltpu.make_async_copy(kv_hbm[i], kv_in.at[i], sems.at[i]) for i in range(8)]
    for slot in range(16):
        inverse[order_ref[slot]] = slot
    for load in [load_uk, load_uv] + loads:
        load.start()

    for slot in range(16):
        c, e = slot // 2, slot % 2
        row = pl.ds(pl.multiple_of(order_ref[slot] * SPAN, SPAN), SPAN)
        qn[row, :] = x_in[c, e * 64:(e + 1) * 64, :]
        g[row, :] = x_in[c, 128 + e * 64:128 + (e + 1) * 64, :]
        qfull[row, LAT:LAT + ROPE] = x_in[c, 256:320, e * 64:(e + 1) * 64]
    load_uk.wait()
    load_uv.wait()
    uk = uk_in[...]
    qfull[:, 0:LAT] = dot(qn[...], uk, NT).astype(BF16)
    dob[...] = dot(g[...], uv_in[...], NT).astype(BF16)
    for d in range(4):
        for cr in range(2):
            i = d * 2 + cr
            ctx = (block ^ d) * 2 + (core ^ cr)
            loads[i].wait()
            piece = jnp.transpose(kv_in[i], (1, 0))
            for e in range(2):
                row = pl.ds(pl.multiple_of(order_ref[ctx * 2 + e] * SPAN, SPAN), SPAN)
                keys[row, :] = piece[e * 64:(e + 1) * 64, :]
    for b in range(4):
        keyt[:, b * 256:(b + 1) * 256] = jnp.transpose(keys[b * 256:(b + 1) * 256, :], (1, 0))
    seg = seg_ref[...]
    begin = jnp.zeros_like(seg)
    for v in range(1, 4):
        below = jnp.sum((seg < v).astype(jnp.int32), axis=1, keepdims=True)
        begin = jnp.where(seg >= v, below, begin)

    def window(b):
        return max(0, b * 256 - 512), b * 256, b * 256 + 256

    def products(b):
        w0, q0, w1 = window(b)
        kw = keys[w0:w1, :]
        return dot(kw, qfull[q0:w1, :], NT), dot(kw[:, 0:LAT], dob[q0:w1, :], NT)

    def softmax(b, scores, dprobs):
        w0, q0, w1 = window(b)
        width = w1 - w0
        k_at = lax.broadcasted_iota(jnp.int32, (width, 256), 0) + w0
        q_at = lax.broadcasted_iota(jnp.int32, (1, 256), 1) + q0
        visible = (k_at >= begin[:, q0:w1]) & (k_at <= q_at)
        scores = jnp.where(visible, scores, -1e30)
        top = jnp.max(scores, axis=0, keepdims=True)
        ex = jnp.exp2((scores - top) * (SCALE * LOG2E))
        probs = ex * (1.0 / jnp.sum(ex, axis=0, keepdims=True))
        row_dot = jnp.sum(probs * dprobs, axis=0, keepdims=True)
        pb = probs.astype(BF16)
        ds = ((probs * SCALE) * (dprobs - row_dot)).astype(BF16)
        pt[b, 0:width, :] = pb
        dst[b, 0:width, :] = ds

    def outputs(b):
        w0, q0, w1 = window(b)
        width = w1 - w0
        ot[:, q0:w1] = dot(keyt[0:LAT, w0:w1], pt[b, 0:width, :], NN).astype(BF16)
        dq = dot(keyt[:, w0:w1], dst[b, 0:width, :], NN)
        dqt[:, q0:w1] = dq[0:LAT, :].astype(BF16)
        dqr[:, q0:w1] = dq[LAT:, :].astype(BF16)

    flight = products(0)
    for b in range(4):
        following = products(b + 1) if b < 3 else None
        softmax(b, *flight)
        outputs(b)
        flight = following
    duk_ref[...] = dot(dqt[...], qn[...], NN).astype(BF16)
    duv_ref[...] = dot(ot[...], g[...], NN).astype(BF16)
    dqn = dot(dqt[...], uk, TN).astype(BF16)
    dqs[...] = jnp.transpose(dqr[...], (1, 0))

    def home(span):
        slot = inverse[span]
        return slot // 2, slot % 2

    for span in range(16):
        c, e = home(span)
        back_ref[c, pl.ds(pl.multiple_of(576 + e * 64, 64), 64), :] = dqn[span * 64:(span + 1) * 64, :]
    for kb in range(4):
        last = min(kb + 3, 4)
        ds = []
        pb = []
        for b in range(kb, last):
            at = kb * 256 - max(0, b * 256 - 512)
            ds.append(dst[b, at:at + 256, :])
            pb.append(pt[b, at:at + 256, :])
        ds = jnp.concatenate(ds, axis=1)
        pb = jnp.concatenate(pb, axis=1)
        lo, hi = kb * 256, last * 256
        part = (dot(ds, qfull[lo:hi, 0:LAT], NN) + dot(pb, dob[lo:hi, :], NN)).astype(BF16)
        dkr[lo:lo + 256, :] = dot(ds, qfull[lo:hi, LAT:], NN).astype(BF16)
        for t in range(4):
            c, e = home(kb * 4 + t)
            for j in range(4):
                row = pl.ds(pl.multiple_of(j * 128 + e * 64, 64), 64)
                back_ref[c, row, :] = part[t * 64:(t + 1) * 64, j * 128:(j + 1) * 128]
    for slot in range(16):
        c, e = slot // 2, slot % 2
        row = pl.ds(pl.multiple_of(order_ref[slot] * SPAN, SPAN), SPAN)
        back_ref[c, 704:768, e * 64:(e + 1) * 64] = dqs[row, :]
        back_ref[c, 512:576, e * 64:(e + 1) * 64] = dkr[row, :]


def attend(order, x, kvs, w_uk, w_uv, seg):
    hbm = pl.BlockSpec(memory_space=pl.ANY)
    vmem = pl.BlockSpec(memory_space=pltpu.VMEM)
    outs = [(8, 768, 128), (512, 128), (512, 128)]
    return pl.pallas_call(
        attend_kernel,
        in_specs=[pl.BlockSpec(memory_space=pltpu.SMEM), vmem] + [hbm] * 10 + [vmem],
        out_specs=[vmem] * 3,
        scratch_shapes=[
            pltpu.VMEM((8, 576, 128), BF16),
            pltpu.VMEM((LAT, 128), BF16),
            pltpu.VMEM((LAT, 128), BF16),
            pltpu.VMEM((SEQ, 576), BF16),
            pltpu.VMEM((576, SEQ), BF16),
            pltpu.VMEM((SEQ, 576), BF16),
            pltpu.VMEM((SEQ, 128), BF16),
            pltpu.VMEM((SEQ, 128), BF16),
            pltpu.VMEM((SEQ, LAT), BF16),
            pltpu.VMEM((4, 768, 256), BF16),
            pltpu.VMEM((4, 768, 256), BF16),
            pltpu.VMEM((LAT, SEQ), BF16),
            pltpu.VMEM((LAT, SEQ), BF16),
            pltpu.VMEM((64, SEQ), BF16),
            pltpu.VMEM((SEQ, ROPE), BF16),
            pltpu.VMEM((SEQ, ROPE), BF16),
            pltpu.SMEM((16,), jnp.int32),
            pltpu.SemaphoreType.DMA((11,)),
        ],
        out_shape=[jax.ShapeDtypeStruct(shape, BF16) for shape in outs],
        compiler_params=pltpu.CompilerParams(vmem_limit_bytes=36 * MIB),
        cost_estimate=pl.CostEstimate(flops=9_000_000_000, bytes_accessed=12 * MIB, transcendentals=600_000),
        name="attend",
    )(order, x, *kvs, w_uk, w_uv, seg)


def call(kernel, name, out, *args):
    return pl.pallas_call(
        kernel,
        out_shape=out,
        compiler_params=pltpu.CompilerParams(vmem_limit_bytes=16 * MIB),
        cost_estimate=pl.CostEstimate(flops=0, bytes_accessed=3 * MIB, transcendentals=0),
        name=name,
    )(*args)


def add1_kernel(a_ref, b_ref, out_ref):
    out_ref[...] = (a_ref[...].astype(F32) + b_ref[...].astype(F32)).astype(BF16)


def add2_kernel(a_ref, b_ref, c_ref, d_ref, uk_ref, uv_ref):
    uk_ref[...] = (a_ref[...].astype(F32) + b_ref[...].astype(F32)).astype(BF16)
    uv_ref[...] = (c_ref[...].astype(F32) + d_ref[...].astype(F32)).astype(BF16)


def add_join_kernel(a_ref, b_ref, c_ref, d_ref, out_ref):
    add2_kernel(a_ref, b_ref, c_ref, d_ref, out_ref.at[0:512, :], out_ref.at[512:1024, :])


def sum_ctx_kernel(x_ref, out_ref):
    total = x_ref[0].astype(F32)
    for i in range(1, 8):
        total = total + x_ref[i].astype(F32)
    total = total.astype(BF16)
    for i in range(8):
        for j in range(4):
            out_ref[i, :, j * 128:(j + 1) * 128] = total[j * 128 + i * 16:j * 128 + (i + 1) * 16, :]
        lane = (i // 4) * 64
        low = 512 + (i % 4) * 16
        out_ref[i, :, 512:576] = total[low:low + 16, lane:lane + 64]
        out_ref[i, :, 576:640] = jnp.zeros((16, 64), BF16)


def sum_ctx(x):
    return pl.pallas_call(
        sum_ctx_kernel,
        grid=(1,),
        in_specs=[pl.BlockSpec((8, 576, 128), lambda i: (0, 0, 0))],
        out_specs=pl.BlockSpec((8, 16, 640), lambda i: (0, 0, 0)),
        out_shape=jax.ShapeDtypeStruct((8, 16, 640), BF16),
        compiler_params=pltpu.CompilerParams(vmem_limit_bytes=16 * MIB),
        name="sum_ctx",
    )(x)


def sum_head_kernel(x_ref, out_ref):
    total = x_ref[0].astype(F32)
    for i in range(1, 8):
        total = total + x_ref[i].astype(F32)
    out_ref[0] = total[:, 0:576].astype(BF16)


def unpack_kernel(x_ref, qn_ref, qr_ref):
    for h in range(8):
        qn_ref[0, :, h * 128:(h + 1) * 128] = x_ref[h, 0:128, :]
        qr_ref[0, 0:64, h * 64:(h + 1) * 64] = x_ref[h, 128:192, 0:64]
        qr_ref[0, 64:128, h * 64:(h + 1) * 64] = x_ref[h, 128:192, 64:128]


def unpack(x):
    return pl.pallas_call(
        unpack_kernel,
        grid=(1,),
        in_specs=[pl.BlockSpec((8, 192, 128), lambda i: (0, 3, 0))],
        out_specs=[
            pl.BlockSpec((1, 128, 1024), lambda i: (0, 0, 0)),
            pl.BlockSpec((1, 128, 512), lambda i: (0, 0, 0)),
        ],
        out_shape=(
            jax.ShapeDtypeStruct((1, 128, 1024), BF16),
            jax.ShapeDtypeStruct((1, 128, 512), BF16),
        ),
        compiler_params=pltpu.CompilerParams(vmem_limit_bytes=16 * MIB),
        name="unpack",
    )(x)


def widen_kernel(*refs):
    uk_ref, uv_ref = refs[8:]
    y = lax.axis_index("y")
    core = lax.axis_index("core")
    for d in range(4):

        @pl.when(pl.program_id(0) == (y ^ d))
        def _():
            for cr in range(2):
                ref = refs[d * 2 + cr]
                at = pl.ds(pl.multiple_of((core ^ cr) * 128, 128), 128)
                uk_ref[:, at] = ref[0:512, :].astype(F32)
                uv_ref[:, at] = ref[512:1024, :].astype(F32)


def widen(pieces):
    piece = pl.BlockSpec((1024, 128), lambda i: (0, 0))
    out = pl.BlockSpec((512, 256), lambda i: (0, i))
    return pl.pallas_call(
        widen_kernel,
        grid=(4,),
        in_specs=[piece] * 8,
        out_specs=[out, out],
        out_shape=(jax.ShapeDtypeStruct((512, 1024), F32),) * 2,
        compiler_params=pltpu.CompilerParams(vmem_limit_bytes=16 * MIB),
        name="widen",
    )(*pieces)


SIZES = {"core": 2, "x": 4, "y": 4, "dp": 4}


def across(x, axis, step):
    return lax.ppermute(x, axis, [(i, i ^ step) for i in range(SIZES[axis])])


def local(q_nope, q_rope, kv_latent, d_out, w_uk, w_uv, segment_ids, span_order):
    kvt = kv_latent[0].T
    skew = [(i * 4 + j, (i ^ j) * 4 + j) for i in range(4) for j in range(4)]
    first = lax.ppermute(kvt, ("y", "x"), skew)
    kvs = []
    for piece in [first] + [across(first, "x", d) for d in (1, 2, 3)]:
        kvs += [piece, across(piece, "core", 1)]
    send = pack(q_nope, q_rope, d_out, kvt)
    send, first = lax.optimization_barrier((send, first))
    x = lax.all_to_all(send, ("y", "core"), 0, 0, tiled=True)
    back, duk, duv = attend(span_order, x, kvs, w_uk, w_uv, segment_ids)
    back = lax.all_to_all(back, ("y", "core"), 0, 0, tiled=True)
    dq_nope, dq_rope = unpack(back)
    parts = lax.all_to_all(sum_ctx(back), ("zl", "x"), 0, 0, tiled=True)
    d_kv = call(sum_head_kernel, "sum_head", jax.ShapeDtypeStruct((1, 16, 576), BF16), parts)
    pair = [jax.ShapeDtypeStruct((512, 128), BF16)] * 2
    duk = call(add1_kernel, "add_uk", pair[0], duk, across(duk, "dp", 1))
    duv = call(add1_kernel, "add_uv", pair[0], duv, across(duv, "dp", 3))
    whole = jax.ShapeDtypeStruct((1024, 128), BF16)
    whole = call(add_join_kernel, "add_join", whole, duk, across(duk, "dp", 3), duv, across(duv, "dp", 1))
    pieces = []
    for piece in [whole] + [across(whole, "y", d) for d in (1, 2, 3)]:
        pieces += [piece, across(piece, "core", 1)]
    pieces[-1], dq_nope, dq_rope = lax.optimization_barrier((pieces[-1], dq_nope, dq_rope))
    dw_uk, dw_uv = widen(pieces)
    return dq_nope, dq_rope, d_kv, dw_uk, dw_uv


def solution(mesh):
    split = Mesh(mesh.devices.reshape(4, 4, 2, 2, 4), ("dp", "y", "core", "zl", "x"))
    ctx = ("y", "core")
    head = ("zl", "x")
    return jax.shard_map(
        local,
        mesh=split,
        in_specs=(
            P("dp", ctx, head),
            P("dp", ctx, head),
            P("dp", ctx, None),
            P("dp", ctx, head),
            P(None, head),
            P(None, head),
            P("dp", None),
            P(),
        ),
        out_specs=(
            P("dp", ctx, head),
            P("dp", ctx, head),
            P("dp", ctx + head, None),
            P(None, head),
            P(None, head),
        ),
        check_vma=False,
    )
```

```python
import jax
import jax.numpy as jnp
from jax import lax
from jax.experimental import pallas as pl
from jax.experimental.pallas import tpu as pltpu
from jax.sharding import Mesh, PartitionSpec as P

LAT = 512
ROPE = 64
NOPE = 128
VDIM = 128
SEQ = 1024
SPAN = 64
SCALE = (NOPE + ROPE) ** -0.5
F32 = jnp.float32
BF16 = jnp.bfloat16
MIB = 1 << 20
LOG2E = 1.4426950408889634


def dot(a, b, dims):
    return lax.dot_general(a, b, (dims, ((), ())), preferred_element_type=F32)


NN = ((1,), (0,))
NT = ((1,), (1,))
TN = ((0,), (0,))


def pack_kernel(qn_ref, qr_ref, do_ref, kv_ref, *out_refs):
    y = lax.axis_index("y")
    core = lax.axis_index("core")
    for d in range(4):
        out = out_refs[d]
        both = pl.ds(pl.multiple_of((y ^ d) * 128, 128), 128)
        ropes = qr_ref[0, :, both]
        for cr in range(2):
            head = pl.ds(pl.multiple_of(((y ^ d) * 2 + (core ^ cr)) * 128, 128), 128)
            at = cr * 320
            out[at:at + 128, :] = qn_ref[0, :, head]
            out[at + 128:at + 256, :] = do_ref[0, :, head]
            rope = jnp.where(core == cr, ropes[:, 0:64], ropes[:, 64:128])
            out[at + 256:at + 320, 0:64] = rope[0:64, :]
            out[at + 256:at + 320, 64:128] = rope[64:128, :]
        out[640:1216, :] = kv_ref[...]


def pack(q_nope, q_rope, d_out, kvt):
    whole = pl.BlockSpec(memory_space=pltpu.VMEM)
    return pl.pallas_call(
        pack_kernel,
        in_specs=[whole] * 4,
        out_specs=[whole] * 4,
        out_shape=[jax.ShapeDtypeStruct((1216, 128), BF16)] * 4,
        compiler_params=pltpu.CompilerParams(vmem_limit_bytes=60 * MIB),
        cost_estimate=pl.CostEstimate(flops=0, bytes_accessed=5 * MIB, transcendentals=0),
        name="pack",
    )(q_nope, q_rope, d_out, kvt)


def attend_kernel(order_ref, *refs):
    parts_hbm = refs[:8]
    uk_hbm, uv_hbm, seg_ref = refs[8:11]
    back_ref = refs[11]
    duk_ref, duv_ref = refs[12:14]
    x_in, kv_in, uk_in, uv_in, keys, keyt, qfull, qn, g, dob, pt, dst, ot, dqt, dqr, dqs, dkr, inverse, sems = refs[14:]
    y = lax.axis_index("y")
    core = lax.axis_index("core")
    me = y * 2 + core
    cols = pl.ds(pl.multiple_of(me * 128, 128), 128)

    load_uk = pltpu.make_async_copy(uk_hbm.at[:, cols], uk_in, sems.at[16])
    load_uv = pltpu.make_async_copy(uv_hbm.at[:, cols], uv_in, sems.at[17])
    load_x = []
    load_kv = []
    for i in range(8):
        at = (i % 2) * 320
        load_x.append(pltpu.make_async_copy(parts_hbm[i].at[at:at + 320, :], x_in.at[i], sems.at[i]))
        load_kv.append(pltpu.make_async_copy(parts_hbm[i].at[640:1216, :], kv_in.at[i], sems.at[8 + i]))
    for load in [load_uk, load_uv] + load_x + load_kv:
        load.start()
    for slot in range(16):
        inverse[order_ref[slot]] = slot

    def place(i, e):
        return pl.ds(pl.multiple_of(order_ref[(me ^ i) * 2 + e] * SPAN, SPAN), SPAN)

    for i in range(8):
        load_x[i].wait()
        for e in range(2):
            row = place(i, e)
            qn[row, :] = x_in[i, e * 64:(e + 1) * 64, :]
            g[row, :] = x_in[i, 128 + e * 64:128 + (e + 1) * 64, :]
            qfull[row, LAT:LAT + ROPE] = x_in[i, 256:320, e * 64:(e + 1) * 64]
    load_uk.wait()
    load_uv.wait()
    uk = uk_in[...]
    qfull[:, 0:LAT] = dot(qn[...], uk, NT).astype(BF16)
    dob[...] = dot(g[...], uv_in[...], NT).astype(BF16)
    for i in range(8):
        load_kv[i].wait()
        piece = jnp.transpose(kv_in[i], (1, 0))
        for e in range(2):
            keys[place(i, e), :] = piece[e * 64:(e + 1) * 64, :]
    for b in range(4):
        keyt[:, b * 256:(b + 1) * 256] = jnp.transpose(keys[b * 256:(b + 1) * 256, :], (1, 0))
    seg = seg_ref[...]
    begin = jnp.zeros_like(seg)
    for v in range(1, 4):
        below = jnp.sum((seg < v).astype(jnp.int32), axis=1, keepdims=True)
        begin = jnp.where(seg >= v, below, begin)

    def window(b):
        return max(0, b * 256 - 512), b * 256, b * 256 + 256

    def products(b):
        w0, q0, w1 = window(b)
        kw = keys[w0:w1, :]
        return dot(kw, qfull[q0:w1, :], NT), dot(kw[:, 0:LAT], dob[q0:w1, :], NT)

    def softmax(b, scores, dprobs):
        w0, q0, w1 = window(b)
        width = w1 - w0
        k_at = lax.broadcasted_iota(jnp.int32, (width, 256), 0) + w0
        q_at = lax.broadcasted_iota(jnp.int32, (1, 256), 1) + q0
        visible = (k_at >= begin[:, q0:w1]) & (k_at <= q_at)
        scores = jnp.where(visible, scores, -1e30)
        top = jnp.max(scores, axis=0, keepdims=True)
        ex = jnp.exp2((scores - top) * (SCALE * LOG2E))
        probs = ex * (1.0 / jnp.sum(ex, axis=0, keepdims=True))
        row_dot = jnp.sum(probs * dprobs, axis=0, keepdims=True)
        pb = probs.astype(BF16)
        ds = ((probs * SCALE) * (dprobs - row_dot)).astype(BF16)
        pt[b, 0:width, :] = pb
        dst[b, 0:width, :] = ds

    def outputs(b):
        w0, q0, w1 = window(b)
        width = w1 - w0
        ot[:, q0:w1] = dot(keyt[0:LAT, w0:w1], pt[b, 0:width, :], NN).astype(BF16)
        dq = dot(keyt[:, w0:w1], dst[b, 0:width, :], NN)
        dqt[:, q0:w1] = dq[0:LAT, :].astype(BF16)
        dqr[:, q0:w1] = dq[LAT:, :].astype(BF16)

    flight = products(0)
    for b in range(4):
        following = products(b + 1) if b < 3 else None
        softmax(b, *flight)
        outputs(b)
        flight = following
    duk_ref[...] = dot(dqt[...], qn[...], NN).astype(BF16)
    duv_ref[...] = dot(ot[...], g[...], NN).astype(BF16)
    dqn = dot(dqt[...], uk, TN).astype(BF16)
    dqs[...] = jnp.transpose(dqr[...], (1, 0))

    def home(span):
        slot = inverse[span]
        return slot // 2, slot % 2

    for span in range(16):
        c, e = home(span)
        back_ref[c, pl.ds(pl.multiple_of(576 + e * 64, 64), 64), :] = dqn[span * 64:(span + 1) * 64, :]
    for kb in range(4):
        last = min(kb + 3, 4)
        ds = []
        pb = []
        for b in range(kb, last):
            at = kb * 256 - max(0, b * 256 - 512)
            ds.append(dst[b, at:at + 256, :])
            pb.append(pt[b, at:at + 256, :])
        ds = jnp.concatenate(ds, axis=1)
        pb = jnp.concatenate(pb, axis=1)
        lo, hi = kb * 256, last * 256
        part = (dot(ds, qfull[lo:hi, 0:LAT], NN) + dot(pb, dob[lo:hi, :], NN)).astype(BF16)
        dkr[lo:lo + 256, :] = dot(ds, qfull[lo:hi, LAT:], NN).astype(BF16)
        for t in range(4):
            c, e = home(kb * 4 + t)
            for j in range(4):
                row = pl.ds(pl.multiple_of(j * 128 + e * 64, 64), 64)
                back_ref[c, row, :] = part[t * 64:(t + 1) * 64, j * 128:(j + 1) * 128]
    for slot in range(16):
        c, e = slot // 2, slot % 2
        row = pl.ds(pl.multiple_of(order_ref[slot] * SPAN, SPAN), SPAN)
        back_ref[c, 704:768, e * 64:(e + 1) * 64] = dqs[row, :]
        back_ref[c, 512:576, e * 64:(e + 1) * 64] = dkr[row, :]


def attend(order, parts, w_uk, w_uv, seg):
    hbm = pl.BlockSpec(memory_space=pl.ANY)
    vmem = pl.BlockSpec(memory_space=pltpu.VMEM)
    outs = [(8, 768, 128), (512, 128), (512, 128)]
    return pl.pallas_call(
        attend_kernel,
        in_specs=[pl.BlockSpec(memory_space=pltpu.SMEM)] + [hbm] * 10 + [vmem],
        out_specs=[vmem] * 3,
        scratch_shapes=[
            pltpu.VMEM((8, 320, 128), BF16),
            pltpu.VMEM((8, 576, 128), BF16),
            pltpu.VMEM((LAT, 128), BF16),
            pltpu.VMEM((LAT, 128), BF16),
            pltpu.VMEM((SEQ, 576), BF16),
            pltpu.VMEM((576, SEQ), BF16),
            pltpu.VMEM((SEQ, 576), BF16),
            pltpu.VMEM((SEQ, 128), BF16),
            pltpu.VMEM((SEQ, 128), BF16),
            pltpu.VMEM((SEQ, LAT), BF16),
            pltpu.VMEM((4, 768, 256), BF16),
            pltpu.VMEM((4, 768, 256), BF16),
            pltpu.VMEM((LAT, SEQ), BF16),
            pltpu.VMEM((LAT, SEQ), BF16),
            pltpu.VMEM((64, SEQ), BF16),
            pltpu.VMEM((SEQ, ROPE), BF16),
            pltpu.VMEM((SEQ, ROPE), BF16),
            pltpu.SMEM((16,), jnp.int32),
            pltpu.SemaphoreType.DMA((18,)),
        ],
        out_shape=[jax.ShapeDtypeStruct(shape, BF16) for shape in outs],
        compiler_params=pltpu.CompilerParams(vmem_limit_bytes=60 * MIB),
        cost_estimate=pl.CostEstimate(flops=9_000_000_000, bytes_accessed=12 * MIB, transcendentals=600_000),
        name="attend",
    )(order, *parts, w_uk, w_uv, seg)


def call(kernel, name, out, *args):
    return pl.pallas_call(
        kernel,
        out_shape=out,
        compiler_params=pltpu.CompilerParams(vmem_limit_bytes=16 * MIB),
        cost_estimate=pl.CostEstimate(flops=0, bytes_accessed=3 * MIB, transcendentals=0),
        name=name,
    )(*args)


def add1_kernel(a_ref, b_ref, out_ref):
    out_ref[...] = (a_ref[...].astype(F32) + b_ref[...].astype(F32)).astype(BF16)


def add2_kernel(a_ref, b_ref, c_ref, d_ref, uk_ref, uv_ref):
    uk_ref[...] = (a_ref[...].astype(F32) + b_ref[...].astype(F32)).astype(BF16)
    uv_ref[...] = (c_ref[...].astype(F32) + d_ref[...].astype(F32)).astype(BF16)


def add_join_kernel(a_ref, b_ref, c_ref, d_ref, out_ref):
    add2_kernel(a_ref, b_ref, c_ref, d_ref, out_ref.at[0:512, :], out_ref.at[512:1024, :])


def sum_ctx_kernel(x_ref, out_ref):
    total = x_ref[0].astype(F32)
    for i in range(1, 8):
        total = total + x_ref[i].astype(F32)
    total = total.astype(BF16)
    for i in range(8):
        for j in range(4):
            out_ref[i, :, j * 128:(j + 1) * 128] = total[j * 128 + i * 16:j * 128 + (i + 1) * 16, :]
        lane = (i // 4) * 64
        low = 512 + (i % 4) * 16
        out_ref[i, :, 512:576] = total[low:low + 16, lane:lane + 64]
        out_ref[i, :, 576:640] = jnp.zeros((16, 64), BF16)


def sum_ctx(x):
    return pl.pallas_call(
        sum_ctx_kernel,
        grid=(1,),
        in_specs=[pl.BlockSpec((8, 576, 128), lambda i: (0, 0, 0))],
        out_specs=pl.BlockSpec((8, 16, 640), lambda i: (0, 0, 0)),
        out_shape=jax.ShapeDtypeStruct((8, 16, 640), BF16),
        compiler_params=pltpu.CompilerParams(vmem_limit_bytes=16 * MIB),
        name="sum_ctx",
    )(x)


def sum_head_kernel(x_ref, out_ref):
    total = x_ref[0].astype(F32)
    for i in range(1, 8):
        total = total + x_ref[i].astype(F32)
    out_ref[0] = total[:, 0:576].astype(BF16)


def unpack_kernel(x_ref, qn_ref, qr_ref):
    for h in range(8):
        qn_ref[0, :, h * 128:(h + 1) * 128] = x_ref[h, 0:128, :]
        qr_ref[0, 0:64, h * 64:(h + 1) * 64] = x_ref[h, 128:192, 0:64]
        qr_ref[0, 64:128, h * 64:(h + 1) * 64] = x_ref[h, 128:192, 64:128]


def unpack(x):
    return pl.pallas_call(
        unpack_kernel,
        grid=(1,),
        in_specs=[pl.BlockSpec((8, 192, 128), lambda i: (0, 3, 0))],
        out_specs=[
            pl.BlockSpec((1, 128, 1024), lambda i: (0, 0, 0)),
            pl.BlockSpec((1, 128, 512), lambda i: (0, 0, 0)),
        ],
        out_shape=(
            jax.ShapeDtypeStruct((1, 128, 1024), BF16),
            jax.ShapeDtypeStruct((1, 128, 512), BF16),
        ),
        compiler_params=pltpu.CompilerParams(vmem_limit_bytes=16 * MIB),
        name="unpack",
    )(x)


def widen_kernel(*refs):
    uk_ref, uv_ref = refs[8:]
    y = lax.axis_index("y")
    core = lax.axis_index("core")
    for d in range(4):

        @pl.when(pl.program_id(0) == (y ^ d))
        def _():
            for cr in range(2):
                ref = refs[d * 2 + cr]
                at = pl.ds(pl.multiple_of((core ^ cr) * 128, 128), 128)
                uk_ref[:, at] = ref[0:512, :].astype(F32)
                uv_ref[:, at] = ref[512:1024, :].astype(F32)


def widen(pieces):
    piece = pl.BlockSpec((1024, 128), lambda i: (0, 0))
    out = pl.BlockSpec((512, 256), lambda i: (0, i))
    return pl.pallas_call(
        widen_kernel,
        grid=(4,),
        in_specs=[piece] * 8,
        out_specs=[out, out],
        out_shape=(jax.ShapeDtypeStruct((512, 1024), F32),) * 2,
        compiler_params=pltpu.CompilerParams(vmem_limit_bytes=16 * MIB),
        name="widen",
    )(*pieces)


SIZES = {"core": 2, "x": 4, "y": 4, "dp": 4}


def across(x, axis, step):
    return lax.ppermute(x, axis, [(i, i ^ step) for i in range(SIZES[axis])])


def local(q_nope, q_rope, kv_latent, d_out, w_uk, w_uv, segment_ids, span_order):
    sends = pack(q_nope, q_rope, d_out, kv_latent[0].T)
    parts = []
    for piece in [sends[0]] + [across(sends[d], "y", d) for d in (1, 2, 3)]:
        parts += [piece, across(piece, "core", 1)]
    back, duk, duv = attend(span_order, parts, w_uk, w_uv, segment_ids)
    back = lax.all_to_all(back, ("y", "core"), 0, 0, tiled=True)
    dq_nope, dq_rope = unpack(back)
    sums = lax.all_to_all(sum_ctx(back), ("zl", "x"), 0, 0, tiled=True)
    d_kv = call(sum_head_kernel, "sum_head", jax.ShapeDtypeStruct((1, 16, 576), BF16), sums)
    pair = [jax.ShapeDtypeStruct((512, 128), BF16)] * 2
    duk = call(add1_kernel, "add_uk", pair[0], duk, across(duk, "dp", 1))
    duv = call(add1_kernel, "add_uv", pair[0], duv, across(duv, "dp", 3))
    whole = jax.ShapeDtypeStruct((1024, 128), BF16)
    whole = call(add_join_kernel, "add_join", whole, duk, across(duk, "dp", 3), duv, across(duv, "dp", 1))
    pieces = []
    for piece in [whole] + [across(whole, "y", d) for d in (1, 2, 3)]:
        pieces += [piece, across(piece, "core", 1)]
    pieces[-1], dq_nope, dq_rope = lax.optimization_barrier((pieces[-1], dq_nope, dq_rope))
    dw_uk, dw_uv = widen(pieces)
    return dq_nope, dq_rope, d_kv, dw_uk, dw_uv


def solution(mesh):
    split = Mesh(mesh.devices.reshape(4, 4, 2, 2, 4), ("dp", "y", "core", "zl", "x"))
    ctx = ("y", "core")
    head = ("zl", "x")
    return jax.shard_map(
        local,
        mesh=split,
        in_specs=(
            P("dp", ctx, head),
            P("dp", ctx, head),
            P("dp", ctx, None),
            P("dp", ctx, head),
            P(None, head),
            P(None, head),
            P("dp", None),
            P(),
        ),
        out_specs=(
            P("dp", ctx, head),
            P("dp", ctx, head),
            P("dp", ctx + head, None),
            P(None, head),
            P(None, head),
        ),
        check_vma=False,
    )
```

```python
import jax
import jax.numpy as jnp
from jax import lax
from jax.experimental import pallas as pl
from jax.experimental.pallas import tpu as pltpu
from jax.sharding import Mesh, PartitionSpec as P

LAT = 512
ROPE = 64
NOPE = 128
VDIM = 128
SEQ = 1024
SPAN = 64
SCALE = (NOPE + ROPE) ** -0.5
F32 = jnp.float32
BF16 = jnp.bfloat16
MIB = 1 << 20
LOG2E = 1.4426950408889634


def dot(a, b, dims):
    return lax.dot_general(a, b, (dims, ((), ())), preferred_element_type=F32)


NN = ((1,), (0,))
NT = ((1,), (1,))
TN = ((0,), (0,))


def pack_kernel(qn_ref, qr_ref, do_ref, kv_ref, *out_refs):
    y = lax.axis_index("y")
    core = lax.axis_index("core")
    for d in range(4):
        out = out_refs[d]
        both = pl.ds(pl.multiple_of((y ^ d) * 128, 128), 128)
        ropes = qr_ref[0, :, both]
        for cr in range(2):
            head = pl.ds(pl.multiple_of(((y ^ d) * 2 + (core ^ cr)) * 128, 128), 128)
            at = cr * 320
            out[at:at + 128, :] = qn_ref[0, :, head]
            out[at + 128:at + 256, :] = do_ref[0, :, head]
            rope = jnp.where(core == cr, ropes[:, 0:64], ropes[:, 64:128])
            out[at + 256:at + 320, 0:64] = rope[0:64, :]
            out[at + 256:at + 320, 64:128] = rope[64:128, :]
        out[640:1216, :] = kv_ref[...]


def pack(q_nope, q_rope, d_out, kvt):
    whole = pl.BlockSpec(memory_space=pltpu.VMEM)
    return pl.pallas_call(
        pack_kernel,
        in_specs=[whole] * 4,
        out_specs=[whole] * 4,
        out_shape=[jax.ShapeDtypeStruct((1216, 128), BF16)] * 4,
        compiler_params=pltpu.CompilerParams(vmem_limit_bytes=60 * MIB),
        cost_estimate=pl.CostEstimate(flops=0, bytes_accessed=5 * MIB, transcendentals=0),
        name="pack",
    )(q_nope, q_rope, d_out, kvt)


def attend_kernel(order_ref, *refs):
    parts_hbm = refs[:8]
    uk_hbm, uv_hbm, seg_ref = refs[8:11]
    back_ref = refs[11]
    duk_ref, duv_ref = refs[12:14]
    x_in, kv_in, uk_in, uv_in, keys, keyt, qfull, qn, g, dob, pt, dst, ot, dqt, dqr, dqs, dkr, inverse, sems = refs[14:]
    y = lax.axis_index("y")
    core = lax.axis_index("core")
    me = y * 2 + core
    cols = pl.ds(pl.multiple_of(me * 128, 128), 128)

    load_uk = pltpu.make_async_copy(uk_hbm.at[:, cols], uk_in, sems.at[16])
    load_uv = pltpu.make_async_copy(uv_hbm.at[:, cols], uv_in, sems.at[17])
    load_x = []
    load_kv = []
    for i in range(8):
        at = (i % 2) * 320
        load_x.append(pltpu.make_async_copy(parts_hbm[i].at[at:at + 320, :], x_in.at[i], sems.at[i]))
        load_kv.append(pltpu.make_async_copy(parts_hbm[i].at[640:1216, :], kv_in.at[i], sems.at[8 + i]))
    for load in [load_uk, load_uv] + load_x + load_kv:
        load.start()
    for slot in range(16):
        inverse[order_ref[slot]] = slot

    def place(i, e):
        return pl.ds(pl.multiple_of(order_ref[(me ^ i) * 2 + e] * SPAN, SPAN), SPAN)

    for i in range(8):
        load_x[i].wait()
        for e in range(2):
            row = place(i, e)
            qn[row, :] = x_in[i, e * 64:(e + 1) * 64, :]
            g[row, :] = x_in[i, 128 + e * 64:128 + (e + 1) * 64, :]
            qfull[row, LAT:LAT + ROPE] = x_in[i, 256:320, e * 64:(e + 1) * 64]
    load_uk.wait()
    load_uv.wait()
    uk = uk_in[...]
    qfull[:, 0:LAT] = dot(qn[...], uk, NT).astype(BF16)
    dob[...] = dot(g[...], uv_in[...], NT).astype(BF16)
    for i in range(8):
        load_kv[i].wait()
        piece = jnp.transpose(kv_in[i], (1, 0))
        for e in range(2):
            keys[place(i, e), :] = piece[e * 64:(e + 1) * 64, :]
    for b in range(4):
        keyt[:, b * 256:(b + 1) * 256] = jnp.transpose(keys[b * 256:(b + 1) * 256, :], (1, 0))
    seg = seg_ref[...]
    begin = jnp.zeros_like(seg)
    for v in range(1, 4):
        below = jnp.sum((seg < v).astype(jnp.int32), axis=1, keepdims=True)
        begin = jnp.where(seg >= v, below, begin)

    def window(b):
        return max(0, b * 256 - 512), b * 256, b * 256 + 256

    def products(b):
        w0, q0, w1 = window(b)
        kw = keys[w0:w1, :]
        return dot(kw, qfull[q0:w1, :], NT), dot(kw[:, 0:LAT], dob[q0:w1, :], NT)

    def softmax(b, scores, dprobs):
        w0, q0, w1 = window(b)
        width = w1 - w0
        k_at = lax.broadcasted_iota(jnp.int32, (width, 256), 0) + w0
        q_at = lax.broadcasted_iota(jnp.int32, (1, 256), 1) + q0
        visible = (k_at >= begin[:, q0:w1]) & (k_at <= q_at)
        scores = jnp.where(visible, scores, -1e30)
        top = jnp.max(scores, axis=0, keepdims=True)
        ex = jnp.exp2((scores - top) * (SCALE * LOG2E))
        probs = ex * (1.0 / jnp.sum(ex, axis=0, keepdims=True))
        row_dot = jnp.sum(probs * dprobs, axis=0, keepdims=True)
        pb = probs.astype(BF16)
        ds = ((probs * SCALE) * (dprobs - row_dot)).astype(BF16)
        pt[b, 0:width, :] = pb
        dst[b, 0:width, :] = ds

    def outputs(b):
        w0, q0, w1 = window(b)
        width = w1 - w0
        ot[:, q0:w1] = dot(keyt[0:LAT, w0:w1], pt[b, 0:width, :], NN).astype(BF16)
        dq = dot(keyt[:, w0:w1], dst[b, 0:width, :], NN)
        dqt[:, q0:w1] = dq[0:LAT, :].astype(BF16)
        dqr[:, q0:w1] = dq[LAT:, :].astype(BF16)

    flight = products(0)
    for b in range(4):
        following = products(b + 1) if b < 3 else None
        softmax(b, *flight)
        outputs(b)
        flight = following
    duk_ref[...] = dot(dqt[...], qn[...], NN).astype(BF16)
    duv_ref[...] = dot(ot[...], g[...], NN).astype(BF16)
    dqn = dot(dqt[...], uk, TN).astype(BF16)
    dqs[...] = jnp.transpose(dqr[...], (1, 0))

    def home(span):
        slot = inverse[span]
        return slot // 2, slot % 2

    for span in range(16):
        c, e = home(span)
        back_ref[c, pl.ds(pl.multiple_of(576 + e * 64, 64), 64), :] = dqn[span * 64:(span + 1) * 64, :]
    for kb in range(4):
        last = min(kb + 3, 4)
        ds = []
        pb = []
        for b in range(kb, last):
            at = kb * 256 - max(0, b * 256 - 512)
            ds.append(dst[b, at:at + 256, :])
            pb.append(pt[b, at:at + 256, :])
        ds = jnp.concatenate(ds, axis=1)
        pb = jnp.concatenate(pb, axis=1)
        lo, hi = kb * 256, last * 256
        part = (dot(ds, qfull[lo:hi, 0:LAT], NN) + dot(pb, dob[lo:hi, :], NN)).astype(BF16)
        dkr[lo:lo + 256, :] = dot(ds, qfull[lo:hi, LAT:], NN).astype(BF16)
        for t in range(4):
            c, e = home(kb * 4 + t)
            for j in range(4):
                row = pl.ds(pl.multiple_of(j * 128 + e * 64, 64), 64)
                back_ref[c, row, :] = part[t * 64:(t + 1) * 64, j * 128:(j + 1) * 128]
    for slot in range(16):
        c, e = slot // 2, slot % 2
        row = pl.ds(pl.multiple_of(order_ref[slot] * SPAN, SPAN), SPAN)
        back_ref[c, 704:768, e * 64:(e + 1) * 64] = dqs[row, :]
        back_ref[c, 512:576, e * 64:(e + 1) * 64] = dkr[row, :]


def attend(order, parts, w_uk, w_uv, seg):
    hbm = pl.BlockSpec(memory_space=pl.ANY)
    vmem = pl.BlockSpec(memory_space=pltpu.VMEM)
    outs = [(8, 768, 128), (512, 128), (512, 128)]
    return pl.pallas_call(
        attend_kernel,
        in_specs=[pl.BlockSpec(memory_space=pltpu.SMEM)] + [hbm] * 10 + [vmem],
        out_specs=[vmem] * 3,
        scratch_shapes=[
            pltpu.VMEM((8, 320, 128), BF16),
            pltpu.VMEM((8, 576, 128), BF16),
            pltpu.VMEM((LAT, 128), BF16),
            pltpu.VMEM((LAT, 128), BF16),
            pltpu.VMEM((SEQ, 576), BF16),
            pltpu.VMEM((576, SEQ), BF16),
            pltpu.VMEM((SEQ, 576), BF16),
            pltpu.VMEM((SEQ, 128), BF16),
            pltpu.VMEM((SEQ, 128), BF16),
            pltpu.VMEM((SEQ, LAT), BF16),
            pltpu.VMEM((4, 768, 256), BF16),
            pltpu.VMEM((4, 768, 256), BF16),
            pltpu.VMEM((LAT, SEQ), BF16),
            pltpu.VMEM((LAT, SEQ), BF16),
            pltpu.VMEM((64, SEQ), BF16),
            pltpu.VMEM((SEQ, ROPE), BF16),
            pltpu.VMEM((SEQ, ROPE), BF16),
            pltpu.SMEM((16,), jnp.int32),
            pltpu.SemaphoreType.DMA((18,)),
        ],
        out_shape=[jax.ShapeDtypeStruct(shape, BF16) for shape in outs],
        compiler_params=pltpu.CompilerParams(vmem_limit_bytes=60 * MIB),
        cost_estimate=pl.CostEstimate(flops=9_000_000_000, bytes_accessed=12 * MIB, transcendentals=600_000),
        name="attend",
    )(order, *parts, w_uk, w_uv, seg)


def call(kernel, name, out, *args):
    return pl.pallas_call(
        kernel,
        out_shape=out,
        compiler_params=pltpu.CompilerParams(vmem_limit_bytes=16 * MIB),
        cost_estimate=pl.CostEstimate(flops=0, bytes_accessed=3 * MIB, transcendentals=0),
        name=name,
    )(*args)


def add1_kernel(a_ref, b_ref, out_ref):
    out_ref[...] = (a_ref[...].astype(F32) + b_ref[...].astype(F32)).astype(BF16)


def add2_kernel(a_ref, b_ref, c_ref, d_ref, uk_ref, uv_ref):
    uk_ref[...] = (a_ref[...].astype(F32) + b_ref[...].astype(F32)).astype(BF16)
    uv_ref[...] = (c_ref[...].astype(F32) + d_ref[...].astype(F32)).astype(BF16)


def add_join_kernel(a_ref, b_ref, c_ref, d_ref, out_ref):
    add2_kernel(a_ref, b_ref, c_ref, d_ref, out_ref.at[0:512, :], out_ref.at[512:1024, :])


def sum_ctx_kernel(x_ref, out_ref):
    total = x_ref[0].astype(F32)
    for i in range(1, 8):
        total = total + x_ref[i].astype(F32)
    total = total.astype(BF16)
    for i in range(8):
        for j in range(4):
            out_ref[i, :, j * 128:(j + 1) * 128] = total[j * 128 + i * 16:j * 128 + (i + 1) * 16, :]
        lane = (i // 4) * 64
        low = 512 + (i % 4) * 16
        out_ref[i, :, 512:576] = total[low:low + 16, lane:lane + 64]
        out_ref[i, :, 576:640] = jnp.zeros((16, 64), BF16)


def sum_ctx(x):
    return pl.pallas_call(
        sum_ctx_kernel,
        grid=(1,),
        in_specs=[pl.BlockSpec((8, 576, 128), lambda i: (0, 0, 0))],
        out_specs=pl.BlockSpec((8, 16, 640), lambda i: (0, 0, 0)),
        out_shape=jax.ShapeDtypeStruct((8, 16, 640), BF16),
        compiler_params=pltpu.CompilerParams(vmem_limit_bytes=16 * MIB),
        name="sum_ctx",
    )(x)


def sum_head_kernel(x_ref, out_ref):
    total = x_ref[0].astype(F32)
    for i in range(1, 8):
        total = total + x_ref[i].astype(F32)
    out_ref[0] = total[:, 0:576].astype(BF16)


def unpack_kernel(x_ref, qn_ref, qr_ref):
    for h in range(8):
        qn_ref[0, :, h * 128:(h + 1) * 128] = x_ref[h, 0:128, :]
        qr_ref[0, 0:64, h * 64:(h + 1) * 64] = x_ref[h, 128:192, 0:64]
        qr_ref[0, 64:128, h * 64:(h + 1) * 64] = x_ref[h, 128:192, 64:128]


def unpack(x):
    return pl.pallas_call(
        unpack_kernel,
        grid=(1,),
        in_specs=[pl.BlockSpec((8, 192, 128), lambda i: (0, 3, 0))],
        out_specs=[
            pl.BlockSpec((1, 128, 1024), lambda i: (0, 0, 0)),
            pl.BlockSpec((1, 128, 512), lambda i: (0, 0, 0)),
        ],
        out_shape=(
            jax.ShapeDtypeStruct((1, 128, 1024), BF16),
            jax.ShapeDtypeStruct((1, 128, 512), BF16),
        ),
        compiler_params=pltpu.CompilerParams(vmem_limit_bytes=16 * MIB),
        name="unpack",
    )(x)


def widen_kernel(*refs):
    uk_ref, uv_ref = refs[8:]
    y = lax.axis_index("y")
    core = lax.axis_index("core")
    for d in range(4):

        @pl.when(pl.program_id(0) == (y ^ d))
        def _():
            for cr in range(2):
                ref = refs[d * 2 + cr]
                at = pl.ds(pl.multiple_of((core ^ cr) * 128, 128), 128)
                uk_ref[:, at] = ref[0:512, :].astype(F32)
                uv_ref[:, at] = ref[512:1024, :].astype(F32)


def widen(pieces):
    piece = pl.BlockSpec((1024, 128), lambda i: (0, 0))
    out = pl.BlockSpec((512, 256), lambda i: (0, i))
    return pl.pallas_call(
        widen_kernel,
        grid=(4,),
        in_specs=[piece] * 8,
        out_specs=[out, out],
        out_shape=(jax.ShapeDtypeStruct((512, 1024), F32),) * 2,
        compiler_params=pltpu.CompilerParams(vmem_limit_bytes=16 * MIB),
        name="widen",
    )(*pieces)


SIZES = {"core": 2, "x": 4, "y": 4, "dp": 4}


def across(x, axis, step):
    return lax.ppermute(x, axis, [(i, i ^ step) for i in range(SIZES[axis])])


def local(q_nope, q_rope, kv_latent, d_out, w_uk, w_uv, segment_ids, span_order):
    sends = pack(q_nope, q_rope, d_out, kv_latent[0].T)
    parts = []
    for piece in [sends[0]] + [across(sends[d], "y", d) for d in (1, 2, 3)]:
        parts += [piece, across(piece, "core", 1)]
    back, duk, duv = attend(span_order, parts, w_uk, w_uv, segment_ids)
    back = lax.all_to_all(back, ("y", "core"), 0, 0, tiled=True)
    dq_nope, dq_rope = unpack(back)
    own, dq_nope, dq_rope = lax.optimization_barrier((sum_ctx(back), dq_nope, dq_rope))
    sums = lax.all_to_all(own, ("zl", "x"), 0, 0, tiled=True)
    d_kv = call(sum_head_kernel, "sum_head", jax.ShapeDtypeStruct((1, 16, 576), BF16), sums)
    pair = [jax.ShapeDtypeStruct((512, 128), BF16)] * 2
    duk = call(add1_kernel, "add_uk", pair[0], duk, across(duk, "dp", 1))
    duv = call(add1_kernel, "add_uv", pair[0], duv, across(duv, "dp", 3))
    whole = jax.ShapeDtypeStruct((1024, 128), BF16)
    whole = call(add_join_kernel, "add_join", whole, duk, across(duk, "dp", 3), duv, across(duv, "dp", 1))
    pieces = []
    for piece in [whole] + [across(whole, "y", d) for d in (1, 2, 3)]:
        pieces += [piece, across(piece, "core", 1)]
    pieces[-1], d_kv = lax.optimization_barrier((pieces[-1], d_kv))
    dw_uk, dw_uv = widen(pieces)
    return dq_nope, dq_rope, d_kv, dw_uk, dw_uv


def solution(mesh):
    split = Mesh(mesh.devices.reshape(4, 4, 2, 2, 4), ("dp", "y", "core", "zl", "x"))
    ctx = ("y", "core")
    head = ("zl", "x")
    return jax.shard_map(
        local,
        mesh=split,
        in_specs=(
            P("dp", ctx, head),
            P("dp", ctx, head),
            P("dp", ctx, None),
            P("dp", ctx, head),
            P(None, head),
            P(None, head),
            P("dp", None),
            P(),
        ),
        out_specs=(
            P("dp", ctx, head),
            P("dp", ctx, head),
            P("dp", ctx + head, None),
            P(None, head),
            P(None, head),
        ),
        check_vma=False,
    )
```

```python
import jax
import jax.numpy as jnp
from jax import lax
from jax.experimental import pallas as pl
from jax.experimental.pallas import tpu as pltpu
from jax.sharding import Mesh, PartitionSpec as P

LAT = 512
ROPE = 64
NOPE = 128
VDIM = 128
SEQ = 1024
SPAN = 64
SCALE = (NOPE + ROPE) ** -0.5
F32 = jnp.float32
BF16 = jnp.bfloat16
MIB = 1 << 20
LOG2E = 1.4426950408889634


def dot(a, b, dims):
    return lax.dot_general(a, b, (dims, ((), ())), preferred_element_type=F32)


NN = ((1,), (0,))
NT = ((1,), (1,))
TN = ((0,), (0,))


def pack_kernel(qn_ref, qr_ref, do_ref, kv_ref, *out_refs):
    y = lax.axis_index("y")
    core = lax.axis_index("core")
    for d in range(4):
        out = out_refs[d]
        both = pl.ds(pl.multiple_of((y ^ d) * 128, 128), 128)
        ropes = qr_ref[0, :, both]
        for cr in range(2):
            head = pl.ds(pl.multiple_of(((y ^ d) * 2 + (core ^ cr)) * 128, 128), 128)
            at = cr * 320
            out[at:at + 128, :] = qn_ref[0, :, head]
            out[at + 128:at + 256, :] = do_ref[0, :, head]
            rope = jnp.where(core == cr, ropes[:, 0:64], ropes[:, 64:128])
            out[at + 256:at + 320, 0:64] = rope[0:64, :]
            out[at + 256:at + 320, 64:128] = rope[64:128, :]
        out[640:1216, :] = kv_ref[...]


def pack(q_nope, q_rope, d_out, kvt):
    whole = pl.BlockSpec(memory_space=pltpu.VMEM)
    return pl.pallas_call(
        pack_kernel,
        in_specs=[whole] * 4,
        out_specs=[whole] * 4,
        out_shape=[jax.ShapeDtypeStruct((1216, 128), BF16)] * 4,
        compiler_params=pltpu.CompilerParams(vmem_limit_bytes=60 * MIB),
        cost_estimate=pl.CostEstimate(flops=0, bytes_accessed=5 * MIB, transcendentals=0),
        name="pack",
    )(q_nope, q_rope, d_out, kvt)


def attend_kernel(order_ref, *refs):
    parts_hbm = refs[:8]
    uk_hbm, uv_hbm, seg_ref = refs[8:11]
    back_ref = refs[11]
    duk_ref, duv_ref = refs[12:14]
    x_in, kv_in, uk_in, uv_in, keys, keyt, qfull, qn, g, dob, pt, dst, ot, dqt, dqr, dqs, dkr, inverse, sems = refs[14:]
    y = lax.axis_index("y")
    core = lax.axis_index("core")
    me = y * 2 + core
    cols = pl.ds(pl.multiple_of(me * 128, 128), 128)

    load_uk = pltpu.make_async_copy(uk_hbm.at[:, cols], uk_in, sems.at[16])
    load_uv = pltpu.make_async_copy(uv_hbm.at[:, cols], uv_in, sems.at[17])
    load_x = []
    load_kv = []
    for i in range(8):
        at = (i % 2) * 320
        load_x.append(pltpu.make_async_copy(parts_hbm[i].at[at:at + 320, :], x_in.at[i], sems.at[i]))
        load_kv.append(pltpu.make_async_copy(parts_hbm[i].at[640:1216, :], kv_in.at[i], sems.at[8 + i]))
    for load in [load_uk, load_uv] + load_x + load_kv:
        load.start()
    for slot in range(16):
        inverse[order_ref[slot]] = slot

    def place(i, e):
        return pl.ds(pl.multiple_of(order_ref[(me ^ i) * 2 + e] * SPAN, SPAN), SPAN)

    for i in range(8):
        load_x[i].wait()
        for e in range(2):
            row = place(i, e)
            qn[row, :] = x_in[i, e * 64:(e + 1) * 64, :]
            g[row, :] = x_in[i, 128 + e * 64:128 + (e + 1) * 64, :]
            qfull[row, LAT:LAT + ROPE] = x_in[i, 256:320, e * 64:(e + 1) * 64]
    load_uk.wait()
    load_uv.wait()
    uk = uk_in[...]
    qfull[:, 0:LAT] = dot(qn[...], uk, NT).astype(BF16)
    dob[...] = dot(g[...], uv_in[...], NT).astype(BF16)
    for i in range(8):
        load_kv[i].wait()
        piece = jnp.transpose(kv_in[i], (1, 0))
        for e in range(2):
            keys[place(i, e), :] = piece[e * 64:(e + 1) * 64, :]
    for b in range(4):
        keyt[:, b * 256:(b + 1) * 256] = jnp.transpose(keys[b * 256:(b + 1) * 256, :], (1, 0))
    seg = seg_ref[...]
    begin = jnp.zeros_like(seg)
    for v in range(1, 4):
        below = jnp.sum((seg < v).astype(jnp.int32), axis=1, keepdims=True)
        begin = jnp.where(seg >= v, below, begin)

    def window(b):
        return max(0, b * 256 - 512), b * 256, b * 256 + 256

    def products(b):
        w0, q0, w1 = window(b)
        kw = keys[w0:w1, :]
        return dot(kw, qfull[q0:w1, :], NT), dot(kw[:, 0:LAT], dob[q0:w1, :], NT)

    def softmax(b, scores, dprobs):
        w0, q0, w1 = window(b)
        width = w1 - w0
        k_at = lax.broadcasted_iota(jnp.int32, (width, 256), 0) + w0
        q_at = lax.broadcasted_iota(jnp.int32, (1, 256), 1) + q0
        visible = (k_at >= begin[:, q0:w1]) & (k_at <= q_at)
        scores = jnp.where(visible, scores, -1e30)
        top = jnp.max(scores, axis=0, keepdims=True)
        ex = jnp.exp2((scores - top) * (SCALE * LOG2E))
        probs = ex * (1.0 / jnp.sum(ex, axis=0, keepdims=True))
        row_dot = jnp.sum(probs * dprobs, axis=0, keepdims=True)
        pb = probs.astype(BF16)
        ds = ((probs * SCALE) * (dprobs - row_dot)).astype(BF16)
        pt[b, 0:width, :] = pb
        dst[b, 0:width, :] = ds

    def outputs(b):
        w0, q0, w1 = window(b)
        width = w1 - w0
        ot[:, q0:w1] = dot(keyt[0:LAT, w0:w1], pt[b, 0:width, :], NN).astype(BF16)
        dq = dot(keyt[:, w0:w1], dst[b, 0:width, :], NN)
        dqt[:, q0:w1] = dq[0:LAT, :].astype(BF16)
        dqr[:, q0:w1] = dq[LAT:, :].astype(BF16)

    flight = products(0)
    for b in range(4):
        following = products(b + 1) if b < 3 else None
        if b > 0:
            outputs(b - 1)
        softmax(b, *flight)
        flight = following
    outputs(3)
    duk_ref[...] = dot(dqt[...], qn[...], NN).astype(BF16)
    duv_ref[...] = dot(ot[...], g[...], NN).astype(BF16)
    dqn = dot(dqt[...], uk, TN).astype(BF16)
    dqs[...] = jnp.transpose(dqr[...], (1, 0))

    def home(span):
        slot = inverse[span]
        return slot // 2, slot % 2

    for span in range(16):
        c, e = home(span)
        back_ref[c, pl.ds(pl.multiple_of(576 + e * 64, 64), 64), :] = dqn[span * 64:(span + 1) * 64, :]
    for kb in range(4):
        last = min(kb + 3, 4)
        ds = []
        pb = []
        for b in range(kb, last):
            at = kb * 256 - max(0, b * 256 - 512)
            ds.append(dst[b, at:at + 256, :])
            pb.append(pt[b, at:at + 256, :])
        ds = jnp.concatenate(ds, axis=1)
        pb = jnp.concatenate(pb, axis=1)
        lo, hi = kb * 256, last * 256
        part = (dot(ds, qfull[lo:hi, 0:LAT], NN) + dot(pb, dob[lo:hi, :], NN)).astype(BF16)
        dkr[lo:lo + 256, :] = dot(ds, qfull[lo:hi, LAT:], NN).astype(BF16)
        for t in range(4):
            c, e = home(kb * 4 + t)
            for j in range(4):
                row = pl.ds(pl.multiple_of(j * 128 + e * 64, 64), 64)
                back_ref[c, row, :] = part[t * 64:(t + 1) * 64, j * 128:(j + 1) * 128]
    for slot in range(16):
        c, e = slot // 2, slot % 2
        row = pl.ds(pl.multiple_of(order_ref[slot] * SPAN, SPAN), SPAN)
        back_ref[c, 704:768, e * 64:(e + 1) * 64] = dqs[row, :]
        back_ref[c, 512:576, e * 64:(e + 1) * 64] = dkr[row, :]


def attend(order, parts, w_uk, w_uv, seg):
    hbm = pl.BlockSpec(memory_space=pl.ANY)
    vmem = pl.BlockSpec(memory_space=pltpu.VMEM)
    outs = [(8, 768, 128), (512, 128), (512, 128)]
    return pl.pallas_call(
        attend_kernel,
        in_specs=[pl.BlockSpec(memory_space=pltpu.SMEM)] + [hbm] * 10 + [vmem],
        out_specs=[vmem] * 3,
        scratch_shapes=[
            pltpu.VMEM((8, 320, 128), BF16),
            pltpu.VMEM((8, 576, 128), BF16),
            pltpu.VMEM((LAT, 128), BF16),
            pltpu.VMEM((LAT, 128), BF16),
            pltpu.VMEM((SEQ, 576), BF16),
            pltpu.VMEM((576, SEQ), BF16),
            pltpu.VMEM((SEQ, 576), BF16),
            pltpu.VMEM((SEQ, 128), BF16),
            pltpu.VMEM((SEQ, 128), BF16),
            pltpu.VMEM((SEQ, LAT), BF16),
            pltpu.VMEM((4, 768, 256), BF16),
            pltpu.VMEM((4, 768, 256), BF16),
            pltpu.VMEM((LAT, SEQ), BF16),
            pltpu.VMEM((LAT, SEQ), BF16),
            pltpu.VMEM((64, SEQ), BF16),
            pltpu.VMEM((SEQ, ROPE), BF16),
            pltpu.VMEM((SEQ, ROPE), BF16),
            pltpu.SMEM((16,), jnp.int32),
            pltpu.SemaphoreType.DMA((18,)),
        ],
        out_shape=[jax.ShapeDtypeStruct(shape, BF16) for shape in outs],
        compiler_params=pltpu.CompilerParams(vmem_limit_bytes=60 * MIB),
        cost_estimate=pl.CostEstimate(flops=9_000_000_000, bytes_accessed=12 * MIB, transcendentals=600_000),
        name="attend",
    )(order, *parts, w_uk, w_uv, seg)


def call(kernel, name, out, *args):
    return pl.pallas_call(
        kernel,
        out_shape=out,
        compiler_params=pltpu.CompilerParams(vmem_limit_bytes=16 * MIB),
        cost_estimate=pl.CostEstimate(flops=0, bytes_accessed=3 * MIB, transcendentals=0),
        name=name,
    )(*args)


def add1_kernel(a_ref, b_ref, out_ref):
    out_ref[...] = (a_ref[...].astype(F32) + b_ref[...].astype(F32)).astype(BF16)


def add2_kernel(a_ref, b_ref, c_ref, d_ref, uk_ref, uv_ref):
    uk_ref[...] = (a_ref[...].astype(F32) + b_ref[...].astype(F32)).astype(BF16)
    uv_ref[...] = (c_ref[...].astype(F32) + d_ref[...].astype(F32)).astype(BF16)


def add_join_kernel(a_ref, b_ref, c_ref, d_ref, out_ref):
    add2_kernel(a_ref, b_ref, c_ref, d_ref, out_ref.at[0:512, :], out_ref.at[512:1024, :])


def sum_ctx_kernel(x_ref, out_ref):
    total = x_ref[0].astype(F32)
    for i in range(1, 8):
        total = total + x_ref[i].astype(F32)
    total = total.astype(BF16)
    for i in range(8):
        for j in range(4):
            out_ref[i, :, j * 128:(j + 1) * 128] = total[j * 128 + i * 16:j * 128 + (i + 1) * 16, :]
        lane = (i // 4) * 64
        low = 512 + (i % 4) * 16
        out_ref[i, :, 512:576] = total[low:low + 16, lane:lane + 64]
        out_ref[i, :, 576:640] = jnp.zeros((16, 64), BF16)


def sum_ctx(x):
    return pl.pallas_call(
        sum_ctx_kernel,
        grid=(1,),
        in_specs=[pl.BlockSpec((8, 576, 128), lambda i: (0, 0, 0))],
        out_specs=pl.BlockSpec((8, 16, 640), lambda i: (0, 0, 0)),
        out_shape=jax.ShapeDtypeStruct((8, 16, 640), BF16),
        compiler_params=pltpu.CompilerParams(vmem_limit_bytes=16 * MIB),
        name="sum_ctx",
    )(x)


def sum_head_kernel(x_ref, out_ref):
    total = x_ref[0].astype(F32)
    for i in range(1, 8):
        total = total + x_ref[i].astype(F32)
    out_ref[0] = total[:, 0:576].astype(BF16)


def unpack_kernel(x_ref, qn_ref, qr_ref):
    for h in range(8):
        qn_ref[0, :, h * 128:(h + 1) * 128] = x_ref[h, 0:128, :]
        qr_ref[0, 0:64, h * 64:(h + 1) * 64] = x_ref[h, 128:192, 0:64]
        qr_ref[0, 64:128, h * 64:(h + 1) * 64] = x_ref[h, 128:192, 64:128]


def unpack(x):
    return pl.pallas_call(
        unpack_kernel,
        grid=(1,),
        in_specs=[pl.BlockSpec((8, 192, 128), lambda i: (0, 3, 0))],
        out_specs=[
            pl.BlockSpec((1, 128, 1024), lambda i: (0, 0, 0)),
            pl.BlockSpec((1, 128, 512), lambda i: (0, 0, 0)),
        ],
        out_shape=(
            jax.ShapeDtypeStruct((1, 128, 1024), BF16),
            jax.ShapeDtypeStruct((1, 128, 512), BF16),
        ),
        compiler_params=pltpu.CompilerParams(vmem_limit_bytes=16 * MIB),
        name="unpack",
    )(x)


def widen_kernel(*refs):
    uk_ref, uv_ref = refs[8:]
    y = lax.axis_index("y")
    core = lax.axis_index("core")
    for d in range(4):

        @pl.when(pl.program_id(0) == (y ^ d))
        def _():
            for cr in range(2):
                ref = refs[d * 2 + cr]
                at = pl.ds(pl.multiple_of((core ^ cr) * 128, 128), 128)
                uk_ref[:, at] = ref[0:512, :].astype(F32)
                uv_ref[:, at] = ref[512:1024, :].astype(F32)


def widen(pieces):
    piece = pl.BlockSpec((1024, 128), lambda i: (0, 0))
    out = pl.BlockSpec((512, 256), lambda i: (0, i))
    return pl.pallas_call(
        widen_kernel,
        grid=(4,),
        in_specs=[piece] * 8,
        out_specs=[out, out],
        out_shape=(jax.ShapeDtypeStruct((512, 1024), F32),) * 2,
        compiler_params=pltpu.CompilerParams(vmem_limit_bytes=16 * MIB),
        name="widen",
    )(*pieces)


SIZES = {"core": 2, "x": 4, "y": 4, "dp": 4}


def across(x, axis, step):
    return lax.ppermute(x, axis, [(i, i ^ step) for i in range(SIZES[axis])])


def local(q_nope, q_rope, kv_latent, d_out, w_uk, w_uv, segment_ids, span_order):
    sends = pack(q_nope, q_rope, d_out, kv_latent[0].T)
    parts = []
    for piece in [sends[0]] + [across(sends[d], "y", d) for d in (1, 2, 3)]:
        parts += [piece, across(piece, "core", 1)]
    back, duk, duv = attend(span_order, parts, w_uk, w_uv, segment_ids)
    back = lax.all_to_all(back, ("y", "core"), 0, 0, tiled=True)
    dq_nope, dq_rope = unpack(back)
    own, dq_nope, dq_rope = lax.optimization_barrier((sum_ctx(back), dq_nope, dq_rope))
    sums = lax.all_to_all(own, ("zl", "x"), 0, 0, tiled=True)
    d_kv = call(sum_head_kernel, "sum_head", jax.ShapeDtypeStruct((1, 16, 576), BF16), sums)
    pair = [jax.ShapeDtypeStruct((512, 128), BF16)] * 2
    duk = call(add1_kernel, "add_uk", pair[0], duk, across(duk, "dp", 1))
    duv = call(add1_kernel, "add_uv", pair[0], duv, across(duv, "dp", 3))
    whole = jax.ShapeDtypeStruct((1024, 128), BF16)
    whole = call(add_join_kernel, "add_join", whole, duk, across(duk, "dp", 3), duv, across(duv, "dp", 1))
    pieces = []
    for piece in [whole] + [across(whole, "y", d) for d in (1, 2, 3)]:
        pieces += [piece, across(piece, "core", 1)]
    dw_uk, dw_uv = widen(pieces)
    return dq_nope, dq_rope, d_kv, dw_uk, dw_uv


def solution(mesh):
    split = Mesh(mesh.devices.reshape(4, 4, 2, 2, 4), ("dp", "y", "core", "zl", "x"))
    ctx = ("y", "core")
    head = ("zl", "x")
    return jax.shard_map(
        local,
        mesh=split,
        in_specs=(
            P("dp", ctx, head),
            P("dp", ctx, head),
            P("dp", ctx, None),
            P("dp", ctx, head),
            P(None, head),
            P(None, head),
            P("dp", None),
            P(),
        ),
        out_specs=(
            P("dp", ctx, head),
            P("dp", ctx, head),
            P("dp", ctx + head, None),
            P(None, head),
            P(None, head),
        ),
        check_vma=False,
    )
```
